256 devices in a mesh: row: 16 (over y_lo, x, core), col: 8 (over z), occ: 2 (over y_hi).
Axes of the slice: x: 4, y: 4 (y_hi: 2, y_lo: 2; y = y_hi * 2 + y_lo), z: 8, core: 2. Of those that a mesh axis runs over, the one named last changes fastest.
Arguments:
- amplitudes: float32 [2, 16, 8, 15488], P(None, 'row', 'col'), may hold values from -6 to 6
- aux_factor: float32 [16, 16, 8, 15488], P('occ', 'row', 'col'), as said below
- virt_irrep: int32 [22], replicated, may hold values from 0 to 7
- pair_irrep: int32 [2], replicated, may hold values from 0 to 7
- aux_irrep: int32 [16], replicated, may hold values from 0 to 7
- block_pattern: int32 [22, 22], replicated, may hold values 0 or 1
Outputs:
- ladder: float32 [2, 16, 8, 15488], P('occ', 'row', 'col')
The draws below stay inside these ranges and needn't reach their ends.
Inputs may be any that keep to these rules, and one draw needn't show every extreme that they name: aux_factor is symmetric in its two virtual indices: B[q, a, c] = B[q, c, a].
All inputs are finite; a program needn't handle non-finite values.
Results may differ from the reference program's by a relative error of at most 0.0001.
Values sent between devices are 32-bit elements; how exact they have to be, the bound alone decides.
A program may use at most 320 MiB of HBM per device.

```python
import jax
import jax.numpy as jnp
from jax import lax

VIRTUALS = 1408
BLOCK_WIDTH = 64
IRREPS = 8
OCC_PAIRS = 2
AUX_FUNCS = 16
VIRT_BLOCKS = 22
ROW_TILES = 16
COL_TILES = 8
LOCAL_CELLS = 15488


def draw_aux_factor(key, part):
    key = jax.random.fold_in(key, 11)
    shape = (AUX_FUNCS, VIRTUALS, VIRTUALS)
    normal_part = jax.random.normal(key, shape, jnp.float32)
    symmetric = (normal_part + jnp.transpose(normal_part, (0, 2, 1))) * 0.7071
    scale_factor = (AUX_FUNCS * VIRTUALS * VIRTUALS * 0.05 / (IRREPS * IRREPS)) ** (-0.25)
    whole = symmetric * scale_factor
    tile_rows = VIRTUALS // ROW_TILES
    sub_width = tile_rows // COL_TILES
    shaped = whole.reshape(AUX_FUNCS, ROW_TILES, tile_rows, ROW_TILES, COL_TILES, sub_width)
    return jnp.transpose(shaped, (0, 1, 4, 2, 3, 5)).reshape(AUX_FUNCS, ROW_TILES, COL_TILES, LOCAL_CELLS)


def set_ends(drawn, stream_key, low, largest):
    extent = drawn.shape
    index_at = [jax.random.randint(jax.random.fold_in(stream_key, axis), (), 0, extent[axis]) for axis in range(len(extent))]
    drawn = drawn.at[tuple(index_at)].set(low)
    longest = extent.index(max(extent))
    index_at[longest] = (index_at[longest] + 1) % extent[longest]
    return drawn.at[tuple(index_at)].set(largest)


def shard_levels(rng, dims, shards, smallest, largest):
    def one(dim, blocks):
        steps = jax.random.uniform(jax.random.fold_in(jax.random.fold_in(rng, 6), dim), (blocks,), jnp.float32, smallest / len(shards), largest / len(shards))
        return jnp.repeat(jnp.exp(steps), dims[dim] // blocks).reshape((-1,) + (1,) * (len(dims) - dim - 1))

    factor_of = one(*shards[0])
    for cut in shards[1:]:
        factor_of = factor_of * one(*cut)
    return factor_of


def normal_values(key, extent, scale, reach, cuts=(), kind=jnp.bfloat16):
    values = scale * jax.random.normal(key, extent, jnp.float32)
    if cuts:
        values = values * shard_levels(key, extent, cuts, -0.22, 0.18)
    return jnp.clip(values, -reach, reach).astype(kind)


def setup_inputs(seed: int = 0) -> dict:
    key_of = jax.random.split(jax.random.key(seed), 7)
    amplitudes = normal_values(key_of[0], (OCC_PAIRS, ROW_TILES, COL_TILES, LOCAL_CELLS), 1.0, 6.0, ((1, 16), (2, 8)), jnp.float32)
    aux_factor = draw_aux_factor(jax.random.fold_in(key_of[6], 71), 0)
    virt_irrep = set_ends(jax.random.randint(key_of[2], (VIRT_BLOCKS,), 0, IRREPS), jax.random.fold_in(key_of[2], 1), 0, IRREPS - 1).astype(jnp.int32)
    pair_irrep = jax.random.randint(key_of[3], (OCC_PAIRS,), 0, IRREPS).astype(jnp.int32)
    aux_irrep = set_ends(jax.random.randint(key_of[4], (AUX_FUNCS,), 0, IRREPS), jax.random.fold_in(key_of[4], 1), 0, IRREPS - 1).astype(jnp.int32)
    block_pattern = set_ends((jax.random.randint(key_of[5], (VIRT_BLOCKS, VIRT_BLOCKS), 0, 3) < 2).astype(jnp.int32), jax.random.fold_in(key_of[5], 1), 0, 1)
    return {"amplitudes": amplitudes, "aux_factor": aux_factor, "virt_irrep": virt_irrep, "pair_irrep": pair_irrep, "aux_irrep": aux_irrep, "block_pattern": block_pattern}


def unpack_layout(stored, leading):
    tile_rows = VIRTUALS // ROW_TILES
    sub_width = tile_rows // COL_TILES
    shaped = stored.reshape(leading, ROW_TILES, COL_TILES, tile_rows, ROW_TILES, sub_width)
    return jnp.transpose(shaped, (0, 1, 3, 4, 2, 5)).reshape(leading, VIRTUALS, VIRTUALS)


def pack_layout(whole, leading):
    tile_rows = VIRTUALS // ROW_TILES
    sub_width = tile_rows // COL_TILES
    shaped = whole.reshape(leading, ROW_TILES, tile_rows, ROW_TILES, COL_TILES, sub_width)
    return jnp.transpose(shaped, (0, 1, 4, 2, 3, 5)).reshape(leading, ROW_TILES, COL_TILES, LOCAL_CELLS)


def reference(amplitudes, aux_factor, virt_irrep, pair_irrep, aux_irrep, block_pattern):
    indices = jnp.arange(VIRTUALS, dtype=jnp.int32)
    blocks = indices // BLOCK_WIDTH
    labels = virt_irrep[blocks]
    product = jnp.bitwise_xor(labels[:, None], labels[None, :])
    kept_mask = product[None] == pair_irrep[:, None, None]
    masked = jnp.where(kept_mask, unpack_layout(amplitudes, OCC_PAIRS), 0.0)
    antisym = masked - jnp.transpose(masked, (0, 2, 1))
    pattern = block_pattern * block_pattern.T
    screen = pattern[blocks][:, blocks] > 0
    aux_mask = jnp.logical_and(screen[None], product[None] == aux_irrep[:, None, None])
    factor = jnp.where(aux_mask, unpack_layout(aux_factor, AUX_FUNCS), 0.0)

    def add_slab(running, aux_slab):
        contracted = jnp.einsum("pcd,db->pcb", antisym, aux_slab, precision=lax.Precision.HIGHEST)
        return running + jnp.einsum("ac,pcb->pab", aux_slab, contracted, precision=lax.Precision.HIGHEST), None

    running, unused = lax.scan(add_slab, jnp.zeros((OCC_PAIRS, VIRTUALS, VIRTUALS), jnp.float32), factor)
    return pack_layout(0.5 * running, OCC_PAIRS)
```

```python
import functools

import jax
import jax.numpy as jnp
import numpy as np
from jax import lax
from jax.experimental import pallas as pl
from jax.experimental.pallas import tpu as pltpu
from jax.sharding import PartitionSpec as P

VIRTUALS = 1408
BLOCK_WIDTH = 64
BLOCKS = 22
LABELS = 8
ROWS, COLS = 16, 8
TILE = 88
WIDE = 176
STRIPS = 11
SLOTS = 64
HALF = 48
NAT = 512
MESH = pl.DeviceIdType.MESH
MIB = 1 << 20
F32, BF16, I32 = jnp.float32, jnp.bfloat16, jnp.int32


def coords():
    return lax.axis_index("row"), lax.axis_index("col"), lax.axis_index("occ")


def iota(shape, dim):
    return lax.broadcasted_iota(I32, shape, dim)


def div11(v):
    return (v * 5958) >> 16


def split(x):
    hi = x.astype(BF16)
    return hi, (x - hi.astype(F32)).astype(BF16)


def dot_nn(a, b):
    return lax.dot_general(a, b, (((1,), (0,)), ((), ())), preferred_element_type=F32)


def dot_nt(a, b):
    return lax.dot_general(a, b, (((1,), (1,)), ((), ())), preferred_element_type=F32)


def cols_before(n, s):
    return (n // TILE) * STRIPS + jnp.clip(n % TILE - STRIPS * s, 0, STRIPS)


def column_facts(virt, s, shape):
    w = iota(shape, 1)
    d = w + 77 * div11(w) + STRIPS * s
    block = d >> 6
    before = [cols_before(BLOCK_WIDTH * b, s) for b in range(BLOCKS + 1)]
    labels = [virt[b] for b in range(BLOCKS)]
    label = jnp.zeros(shape, I32)
    rank = w
    for b in range(BLOCKS):
        base = -before[b]
        for e in range(b):
            base = base + jnp.where(labels[e] == labels[b], before[e + 1] - before[e], 0)
        here = block == b
        label = jnp.where(here, labels[b], label)
        rank = jnp.where(here, w + base, rank)
    return d, block, label, rank


def row_label(virt, block, first):
    label = virt[first]
    for k in (1, 2):
        label = jnp.where(block == first + k, virt[jnp.minimum(first + k, BLOCKS - 1)], label)
    return label


def pack_kernel(virt, pair, aux, pat, a_ref, b_ref, ac_ref, bc_ref, d_ref):
    r, s, o = coords()
    first = (STRIPS * r) >> 3
    d, block, label, rank = column_facts(virt, s, (1, WIDE))
    sel = jnp.where((iota((128, WIDE), 0) & (SLOTS - 1)) == rank, 1.0, 0.0).astype(BF16)
    screens = []
    for k in range(3):
        x = jnp.minimum(first + k, BLOCKS - 1)
        flag = jnp.zeros((1, WIDE), I32)
        for b in range(BLOCKS):
            flag = jnp.where(block == b, pat[x, b] * pat[b, x], flag)
        screens.append(flag)

    row = iota((TILE, 1), 0)
    q = div11(row)
    row_block = (STRIPS * r + row - STRIPS * q) >> 3
    target = row_label(virt, row_block, first)
    aux_row = jnp.zeros((TILE, 1), I32)
    for k in range(8):
        aux_row = jnp.where(q == k, aux[8 * o + k], aux_row)
    target = target ^ aux_row
    screen = jnp.where(
        row_block == first, screens[0], jnp.where(row_block == first + 1, screens[1], screens[2])
    )
    keep_b = jnp.logical_and(label == target, screen > 0)

    row = iota((2 * STRIPS, 1), 0)
    p = jnp.where(row >= STRIPS, 1, 0)
    row_block = (STRIPS * r + row - STRIPS * p) >> 3
    keep_a = label == (row_label(virt, row_block, first) ^ jnp.where(p == 1, pair[1], pair[0]))

    for src, count, base, keep in ((b_ref, 8, 0, keep_b), (a_ref, 2, 8 * TILE, keep_a)):
        n = count * STRIPS
        lines = [src[pl.ds(k, n, stride=STRIPS), :] for k in range(STRIPS)]
        for v in range(8):
            start = WIDE * v
            low, off = start // 128, start % 128
            last = (start + WIDE - 1) // 128
            tile = jnp.concatenate(lines[low : last + 1], axis=1)[:, off : off + WIDE]
            hi, lo = split(jnp.where(keep, tile, 0.0))
            d_ref[pl.ds(base + v, n, stride=8), :] = dot_nt(hi, sel) + dot_nt(lo, sel)
    d_ref[10 * TILE : 10 * TILE + 8, :] = jnp.zeros((8, 128), F32)
    left = iota((HALF, 128), 1) < SLOTS
    for k in range(10):
        top, bottom = d_ref[pl.ds(TILE * k, HALF), :], d_ref[pl.ds(TILE * k + HALF, HALF), :]
        if k < 8:
            bc_ref[k] = jnp.where(left, top, bottom)
        else:
            ac_ref[k - 8] = jnp.where(left, top, bottom)


def gather_kernel(ac_ref, bc_ref, aa_ref, sa_ref, send, recv, near):
    r, s, o = coords()
    c, x, y = r % 2, (r // 2) % 4, r // 8

    def at(cc, xx, yy, ss):
        return (yy * 8 + xx * 2 + cc, ss, o)

    zs = [(at(c, x, y, (s + k) % 8)) for k in range(1, 8)]
    xs = [(at(c, (x + k) % 4, y, s)) for k in range(1, 4)]
    ynear = at(c, x, 1 - y, s)
    sibling = at(1 - c, x, y, s)
    barrier = pltpu.get_barrier_semaphore()
    for peer in zs + xs + [ynear, sibling]:
        pl.semaphore_signal(barrier, inc=1, device_id=peer, device_id_type=MESH)
    pl.semaphore_wait(barrier, 12)

    copies = []

    def put(src, dst, peer, n):
        copy = pltpu.make_async_remote_copy(
            src_ref=src,
            dst_ref=dst,
            send_sem=send.at[n],
            recv_sem=recv.at[n],
            device_id=peer,
            device_id_type=MESH,
        )
        copy.start()
        copies.append(copy)
        return copy

    def arrived(ref, n):
        pltpu.make_async_remote_copy(
            src_ref=ref,
            dst_ref=ref,
            send_sem=send.at[n],
            recv_sem=recv.at[n],
            device_id=sibling,
            device_id_type=MESH,
        ).wait_recv()

    own_a = pltpu.make_async_copy(ac_ref.at[y], aa_ref.at[c, x, y, s], near.at[0])
    own_s = pltpu.make_async_copy(bc_ref.at[s], sa_ref.at[c, x, y, s], near.at[1])
    put(ac_ref.at[1 - y], aa_ref.at[c, x, y, s], ynear, 7)
    for k in range(1, 8):
        put(bc_ref.at[(s + k) % 8], sa_ref.at[c, x, y, s], zs[k - 1], k - 1)
    own_a.start()
    own_s.start()
    own_a.wait()
    arrived(aa_ref.at[c, x, 1 - y, s], 7)
    for k in range(1, 4):
        put(aa_ref.at[c, x, :, s], aa_ref.at[c, x, :, s], xs[k - 1], 7 + k)
    own_s.wait()
    for k in range(1, 8):
        arrived(sa_ref.at[c, x, y, (s - k + 8) % 8], k - 1)
    put(sa_ref.at[c, x, y], sa_ref.at[c, x, y], ynear, 18)
    for k in range(1, 4):
        arrived(aa_ref.at[c, (x - k + 4) % 4, :, s], 7 + k)
    for k in range(1, 8):
        put(aa_ref.at[c, :, :, s], aa_ref.at[c, :, :, s], zs[k - 1], 10 + k)
    put(aa_ref.at[c, :, :, s], aa_ref.at[c, :, :, s], sibling, 26)
    arrived(sa_ref.at[c, x, 1 - y], 18)
    for k in range(1, 4):
        put(sa_ref.at[c, x], sa_ref.at[c, x], xs[k - 1], 18 + k)
    put(sa_ref.at[c, x], sa_ref.at[c, x], sibling, 22)
    for k in range(1, 4):
        xk = (x - k + 4) % 4
        arrived(sa_ref.at[c, xk], 18 + k)
        put(sa_ref.at[c, xk], sa_ref.at[c, xk], sibling, 22 + k)
    for k in range(1, 8):
        sk = (s - k + 8) % 8
        arrived(aa_ref.at[c, :, :, sk], 10 + k)
        put(aa_ref.at[c, :, :, sk], aa_ref.at[c, :, :, sk], sibling, 26 + k)
    arrived(sa_ref.at[1 - c, x], 22)
    for k in range(1, 4):
        arrived(sa_ref.at[1 - c, (x - k + 4) % 4], 22 + k)
    arrived(aa_ref.at[1 - c, :, :, s], 26)
    for k in range(1, 8):
        arrived(aa_ref.at[1 - c, :, :, (s - k + 8) % 8], 26 + k)
    for copy in copies:
        copy.wait_send()


def product_kernel(
    virt, pair, aux, aa_ref, sa_ref, z_ref, a2, s2, v1, v2, zs, whi, wlo, lists, counts
):
    r, s, o = coords()
    core, x_me, pair_me = r % 2, (r // 2) % 4, r // 8
    h = aux[8 * o + s]
    hp = h ^ pair[pair_me]
    left = iota((HALF, 128), 1) < SLOTS

    def unpack(k, _):
        c, x, y = k % 2, (k // 2) % 4, k // 8
        base = pl.multiple_of(k * TILE, 8)
        for src, dst in ((sa_ref, s2), (aa_ref, a2)):
            for j in range(4):
                even, odd = src[c, x, y, 2 * j], src[c, x, y, 2 * j + 1]
                top = jnp.where(left, even, pltpu.roll(odd, SLOTS, 1))
                bottom = jnp.where(left, pltpu.roll(even, SLOTS, 1), odd)
                dst[pl.ds(base, HALF), pl.ds(128 * j, 128)] = top
                dst[pl.ds(base + HALF, TILE - HALF), pl.ds(128 * j, 128)] = bottom[: TILE - HALF]
        return 0

    lax.fori_loop(0, ROWS, unpack, 0)
    for ref in (s2, a2):
        ref[VIRTUALS:, :] = jnp.zeros((BLOCK_WIDTH, NAT), F32)

    for g in range(LABELS):
        counts[g] = 0
        for j in range(8):
            lists[8 * g + j] = BLOCKS
    places = []
    for b in range(BLOCKS):
        g = virt[b]
        n = counts[g]
        lists[8 * g + jnp.minimum(n, 7)] = b
        counts[g] = n + 1
        places.append(n)

    group = iota((8, 1), 0)
    d, block, label, rank = column_facts(virt, group, (8, WIDE))
    place = jnp.zeros((8, WIDE), I32)
    for b in range(BLOCKS):
        place = jnp.where(block == b, places[b], place)
    natural = place * BLOCK_WIDTH + (d & (BLOCK_WIDTH - 1))

    tiles = (2 * x_me + core, 8 + 2 * x_me + core)
    bases = [pl.multiple_of(t * TILE, 8) for t in tiles]
    firsts = [(STRIPS * t) >> 3 for t in tiles]
    row = iota((TILE, 1), 0)
    row_blocks = [(t * TILE + row) >> 6 for t in tiles]
    labels = jnp.concatenate([row_label(virt, b, f) for b, f in zip(row_blocks, firsts)], axis=0)

    def to_natural(x, target):
        hi, lo = split(x)
        both = jnp.concatenate([hi, lo], axis=0)
        target = jnp.concatenate([target, target], axis=0)
        total = jnp.zeros((2 * WIDE, NAT), F32)
        for k in range(8):
            j = k // 2
            spread = jnp.where(
                iota((128, WIDE), 0) == rank[k : k + 1] + SLOTS * (k % 2), 1.0, 0.0
            ).astype(BF16)
            dense = dot_nn(both[:, 128 * j : 128 * j + 128], spread)
            dense = jnp.where(label[k : k + 1] == target, dense, 0.0).astype(BF16)
            pick = jnp.where(iota((NAT, WIDE), 0) == natural[k : k + 1], 1.0, 0.0).astype(BF16)
            total = total + dot_nt(dense, pick)
        return total[:WIDE] + total[WIDE:]

    own = [s2[pl.ds(b, TILE), :] for b in bases]
    own_natural = to_natural(jnp.concatenate(own, axis=0), labels ^ h)

    def load_rows(src, g, half):
        for j in range(4):
            b = lists[8 * g + 4 * half + j]
            hi, lo = split(src[pl.ds(pl.multiple_of(b * BLOCK_WIDTH, BLOCK_WIDTH), BLOCK_WIDTH), :])
            whi[pl.ds(BLOCK_WIDTH * j, BLOCK_WIDTH), :] = hi
            wlo[pl.ds(BLOCK_WIDTH * j, BLOCK_WIDTH), :] = lo

    def dot3(dot, a):
        hi, lo = split(a)
        return dot(hi, whi[...]) + dot(lo, whi[...]) + dot(hi, wlo[...])

    v1[...] = jnp.zeros_like(v1)
    v2[...] = jnp.zeros_like(v2)
    zs[...] = jnp.zeros_like(zs)
    for t in range(2):
        last = (STRIPS * tiles[t] + STRIPS - 1) >> 3

        def first_product(x, _, t=t):
            g1 = virt[x] ^ h
            g2 = virt[x] ^ hp
            here = row_blocks[t] == x
            mine = jnp.where(here, own[t], 0.0)
            mine_natural = jnp.where(here, own_natural[TILE * t : TILE * t + TILE], 0.0)
            for half in range(2):
                part = slice(256 * half, 256 * half + 256)

                @pl.when(counts[g1] > 4 * half)
                def _():
                    load_rows(a2, g1, half)
                    v2[t] += dot3(dot_nn, mine_natural[:, part])

                @pl.when(counts[g2] > 4 * half)
                def _():
                    load_rows(a2, g2, half)
                    v1[t, :, part] += dot3(dot_nt, mine)

            return 0

        lax.fori_loop(firsts[t], last + 1, first_product, 0)

    turned = to_natural(jnp.concatenate([v2[0], v2[1]], axis=0), labels ^ hp)
    for t in range(2):
        last = (STRIPS * tiles[t] + STRIPS - 1) >> 3
        y = turned[TILE * t : TILE * t + TILE] - v1[t]

        def second_product(x, _, t=t, y=y):
            g2 = virt[x] ^ hp
            mine = jnp.where(row_blocks[t] == x, y, 0.0)
            for half in range(2):

                @pl.when(counts[g2] > 4 * half)
                def _():
                    load_rows(s2, g2, half)
                    zs[t, :TILE] += dot3(dot_nn, mine[:, 256 * half : 256 * half + 256])

            return 0

        lax.fori_loop(firsts[t], last + 1, second_product, 0)

    for t in range(2):
        for k in range(8):
            j = k // 2
            top = zs[t, 0:HALF, pl.ds(128 * j, 128)]
            bottom = zs[t, HALF : 2 * HALF, pl.ds(128 * j, 128)]
            if k % 2 == 0:
                z_ref[t, k] = jnp.where(left, top, pltpu.roll(bottom, SLOTS, 1))
            else:
                z_ref[t, k] = jnp.where(left, pltpu.roll(top, SLOTS, 1), bottom)


def scatter_kernel(z_ref, out_ref, send, recv, near):
    r, s, o = coords()
    y, rest = r // 8, r % 8
    alone = jnp.where(y == o, 1, 0)
    barrier = pltpu.get_barrier_semaphore()

    def greet(e, k):
        pl.semaphore_signal(
            barrier, inc=1, device_id=(o * 8 + rest, (s + k) % 8, e), device_id_type=MESH
        )

    def describe(e, k):
        return pltpu.make_async_remote_copy(
            src_ref=z_ref.at[e, (s + k) % 8],
            dst_ref=out_ref.at[o, s],
            send_sem=send.at[8 * e + k],
            recv_sem=recv.at[8 * o + k],
            device_id=(e * 8 + rest, (s + k) % 8, y),
            device_id_type=MESH,
        )

    def sender(e, k):
        describe(e, k).start()

    def receive(e, k):
        spot = out_ref.at[e, (s - k + 8) % 8]
        pltpu.make_async_remote_copy(
            src_ref=spot,
            dst_ref=spot,
            send_sem=send.at[0],
            recv_sem=recv.at[8 * e + k],
            device_id=(o * 8 + rest, (s + 1) % 8, e),
            device_id_type=MESH,
        ).wait_recv()

    def finish(e, k):
        describe(e, k).wait_send()

    def each(fn, mine):
        for k in list(range(1, 8)) + [0]:
            for e in range(2):
                if k:
                    fn(e, k)
                else:
                    pl.when(jnp.logical_or(y != o, mine != e))(functools.partial(fn, e, k))

    each(greet, o)
    pl.semaphore_wait(barrier, 16 - alone)
    each(sender, y)

    @pl.when(y == o)
    def _():
        copy = pltpu.make_async_copy(z_ref.at[y, s], out_ref.at[o, s], near.at[0])
        copy.start()
        copy.wait()

    each(receive, o)
    each(finish, y)


def finish_kernel(virt, pair, parts_ref, out_ref, low_ref, high_ref):
    r, s, o = coords()
    first = (STRIPS * r) >> 3
    d, block, label, rank = column_facts(virt, s, (1, WIDE))
    total = parts_ref[0, 0]
    for k in range(1, 16):
        total = total + parts_ref[k // 8, k % 8]
    hi, lo = split(0.5 * total)
    row = iota((HALF, 1), 0)
    for half in range(2):
        spread = jnp.where(iota((128, WIDE), 0) == rank + SLOTS * half, 1.0, 0.0).astype(BF16)
        dense = dot_nn(hi, spread) + dot_nn(lo, spread)
        row_block = (TILE * r + HALF * half + row) >> 6
        keep = label == (row_label(virt, row_block, first) ^ pair[o])
        dense = jnp.where(keep, dense, 0.0)
        low_ref[HALF * half : HALF * half + HALF, :] = dense[:, :128]
        high_ref[HALF * half : HALF * half + HALF, : WIDE - 128] = dense[:, 128:]
    lines = []
    for v in range(8):
        low, high = low_ref[pl.ds(v, STRIPS, stride=8), :], high_ref[pl.ds(v, STRIPS, stride=8), :]
        lines.append(jnp.concatenate([low, high[:, : WIDE - 128]], axis=1))
    for k in range(STRIPS):
        v, w = (128 * k) // WIDE, (128 * k) % WIDE
        piece = lines[v][:, w : min(WIDE, w + 128)]
        if w + 128 > WIDE:
            piece = jnp.concatenate([piece, lines[v + 1][:, : w + 128 - WIDE]], axis=1)
        out_ref[pl.ds(k, STRIPS, stride=STRIPS), :] = piece


def smem(n):
    return [pl.BlockSpec(memory_space=pltpu.SMEM)] * n


def vmem(n):
    return [pl.BlockSpec(memory_space=pltpu.VMEM)] * n


def anywhere(n):
    return [pl.BlockSpec(memory_space=pl.ANY)] * n


def shape(*dims):
    return jax.ShapeDtypeStruct(dims, F32)


def run_pack(virt, pair, aux, pat, a, b):
    return pl.pallas_call(
        pack_kernel,
        out_shape=(shape(2, HALF, 128), shape(8, HALF, 128)),
        in_specs=smem(4) + vmem(2),
        out_specs=tuple(vmem(2)),
        scratch_shapes=[pltpu.VMEM((10 * TILE + 8, 128), F32)],
        compiler_params=pltpu.CompilerParams(vmem_limit_bytes=32 * MIB),
    )(virt, pair, aux, pat, a, b)


def run_gather(ac, bc):
    full = shape(2, 4, 2, 8, HALF, 128)
    return pl.pallas_call(
        gather_kernel,
        out_shape=(full, full),
        in_specs=anywhere(2),
        out_specs=tuple(anywhere(2)),
        scratch_shapes=[
            pltpu.SemaphoreType.DMA((34,)),
            pltpu.SemaphoreType.DMA((34,)),
            pltpu.SemaphoreType.DMA((2,)),
        ],
        compiler_params=pltpu.CompilerParams(collective_id=0, has_side_effects=True),
    )(ac, bc)


def run_product(virt, pair, aux, aa, sa):
    tall = pltpu.VMEM((VIRTUALS + BLOCK_WIDTH, NAT), F32)
    return pl.pallas_call(
        product_kernel,
        out_shape=shape(2, 8, HALF, 128),
        in_specs=smem(3) + vmem(2),
        out_specs=vmem(1)[0],
        scratch_shapes=[
            tall,
            tall,
            pltpu.VMEM((2, TILE, NAT), F32),
            pltpu.VMEM((2, TILE, NAT), F32),
            pltpu.VMEM((2, 2 * HALF, NAT), F32),
            pltpu.VMEM((256, NAT), BF16),
            pltpu.VMEM((256, NAT), BF16),
            pltpu.SMEM((64,), I32),
            pltpu.SMEM((8,), I32),
        ],
        compiler_params=pltpu.CompilerParams(vmem_limit_bytes=48 * MIB),
    )(virt, pair, aux, aa, sa)


def run_scatter(z):
    return pl.pallas_call(
        scatter_kernel,
        out_shape=shape(2, 8, HALF, 128),
        in_specs=anywhere(1),
        out_specs=anywhere(1)[0],
        scratch_shapes=[
            pltpu.SemaphoreType.DMA((16,)),
            pltpu.SemaphoreType.DMA((16,)),
            pltpu.SemaphoreType.DMA((1,)),
        ],
        compiler_params=pltpu.CompilerParams(collective_id=1, has_side_effects=True),
    )(z)


def run_finish(virt, pair, parts):
    return pl.pallas_call(
        finish_kernel,
        out_shape=shape(121, 128),
        in_specs=smem(2) + vmem(1),
        out_specs=vmem(1)[0],
        scratch_shapes=[pltpu.VMEM((2 * HALF, 128), F32)] * 2,
        compiler_params=pltpu.CompilerParams(vmem_limit_bytes=32 * MIB),
    )(virt, pair, parts)


def packed_path(amplitudes, aux_factor, virt, pair, aux, pat):
    ac, bc = run_pack(virt, pair, aux, pat, amplitudes.reshape(242, 128), aux_factor.reshape(968, 128))
    aa, sa = run_gather(ac, bc)
    z = run_product(virt, pair, aux, aa, sa)
    out = run_finish(virt, pair, run_scatter(z))
    return out.reshape(1, 1, 1, TILE * WIDE)


def labels_fit(virt):
    edges = np.arange(BLOCKS + 1)[:, None] * BLOCK_WIDTH
    before = edges // TILE * STRIPS + np.clip(edges % TILE - STRIPS * np.arange(COLS), 0, STRIPS)
    share = jnp.asarray(before[1:] - before[:-1], I32)
    same = virt[:, None] == jnp.arange(LABELS, dtype=I32)
    totals = jnp.sum(jnp.where(same[:, :, None], share[:, None, :], 0), axis=0)
    return jnp.max(totals) <= SLOTS


def block_onehot(indices, block_count):
    return indices[..., None] // BLOCK_WIDTH == jnp.arange(block_count, dtype=jnp.int32)


def label_lookup(hot_table, virt_irrep):
    return jnp.sum(jnp.where(hot_table, virt_irrep, 0), axis=-1)


def dense_path(amplitudes, aux_factor, virt_irrep, pair_irrep, aux_irrep, block_pattern):
    tile_count = lax.axis_size("row")
    col_count = lax.axis_size("col")
    local_rows = VIRTUALS // tile_count
    sub_width = local_rows // col_count
    amplitudes = amplitudes.reshape(amplitudes.shape[0], local_rows, tile_count, sub_width)
    aux_factor = aux_factor.reshape(aux_factor.shape[0], local_rows, tile_count, sub_width)
    block_count = virt_irrep.shape[0]
    row_index = lax.axis_index("row") * local_rows + jnp.arange(local_rows, dtype=jnp.int32)
    col_index = (
        jnp.arange(tile_count, dtype=jnp.int32)[:, None] * local_rows
        + lax.axis_index("col") * sub_width
        + jnp.arange(sub_width, dtype=jnp.int32)[None, :]
    )
    row_hot = block_onehot(row_index, block_count)
    col_hot = block_onehot(col_index, block_count)
    product = jnp.bitwise_xor(
        label_lookup(row_hot, virt_irrep)[:, None, None], label_lookup(col_hot, virt_irrep)[None]
    )
    kept_mask = product[None] == pair_irrep[:, None, None, None]
    masked = jnp.where(kept_mask, amplitudes, 0.0)
    pattern = (block_pattern * block_pattern.T).astype(jnp.float32)
    screen = (
        jnp.einsum(
            "ak,kl,itl->ait", row_hot.astype(jnp.float32), pattern, col_hot.astype(jnp.float32)
        )
        > 0.5
    )
    aux_here = aux_factor.shape[0]
    aux_labels = lax.dynamic_slice_in_dim(aux_irrep, lax.axis_index("occ") * aux_here, aux_here, 0)
    aux_mask = jnp.logical_and(screen[None], product[None] == aux_labels[:, None, None, None])
    factor = jnp.where(aux_mask, aux_factor, 0.0)
    half_pairs = masked.shape[0] // lax.axis_size("occ")
    masked = lax.dynamic_slice_in_dim(masked, lax.axis_index("occ") * half_pairs, half_pairs, 0)
    factor = lax.all_gather(factor, "occ", axis=0, tiled=True)
    pair_count = masked.shape[0]
    aux_count = factor.shape[0]
    split_view = masked.reshape(pair_count, col_count, sub_width, tile_count, sub_width)
    swapped = lax.all_to_all(
        lax.all_to_all(split_view, "row", split_axis=3, concat_axis=3, tiled=True),
        "col",
        split_axis=1,
        concat_axis=4,
        tiled=True,
    )
    mirrored = swapped.reshape(pair_count, sub_width, tile_count, local_rows).transpose(0, 3, 2, 1)
    antisym = masked - mirrored
    columns = lax.all_gather(factor, "row", axis=1, tiled=True)
    columns = columns.reshape(aux_count, tile_count, local_rows, tile_count * sub_width)
    rows_panel = lax.all_gather(factor, "col", axis=3, tiled=True).reshape(
        aux_count, local_rows, tile_count * local_rows
    )
    chosen = columns
    contracted = jnp.einsum(
        "pcik,qikn->qpcn",
        lax.all_gather(antisym, "col", axis=3, tiled=True),
        chosen,
        precision=lax.Precision.HIGHEST,
    )
    chosen = rows_panel
    summed = lax.psum_scatter(
        jnp.einsum("qca,qpcn->apn", chosen, contracted, precision=lax.Precision.HIGHEST),
        "row",
        scatter_dimension=0,
        tiled=True,
    )
    pairs_out = summed.shape[1]
    result = (
        (0.5 * summed).reshape(local_rows, pairs_out, tile_count, sub_width).transpose(1, 0, 2, 3)
    )
    return result.reshape(pairs_out, 1, 1, local_rows * tile_count * sub_width)


def per_device(*args):
    return lax.cond(labels_fit(args[2]), packed_path, dense_path, *args)


def solution(mesh):
    placed = (P(None, "row", "col", None), P("occ", "row", "col", None), P(), P(), P(), P())
    return jax.shard_map(
        per_device,
        mesh=mesh,
        in_specs=placed,
        out_specs=P("occ", "row", "col", None),
        check_vma=False,
    )
```

```python
import functools

import jax
import jax.numpy as jnp
import numpy as np
from jax import lax
from jax.experimental import pallas as pl
from jax.experimental.pallas import tpu as pltpu
from jax.sharding import PartitionSpec as P

VIRTUALS = 1408
BLOCK_WIDTH = 64
BLOCKS = 22
LABELS = 8
ROWS, COLS = 16, 8
TILE = 88
WIDE = 176
STRIPS = 11
SLOTS = 64
HALF = 48
MESH = pl.DeviceIdType.MESH
MIB = 1 << 20
F32, BF16, I32 = jnp.float32, jnp.bfloat16, jnp.int32


def coords():
    return lax.axis_index("row"), lax.axis_index("col"), lax.axis_index("occ")


def iota(shape, dim):
    return lax.broadcasted_iota(I32, shape, dim)


def div11(v):
    return (v * 5958) >> 16


def split(x):
    hi = x.astype(BF16)
    return hi, (x - hi.astype(F32)).astype(BF16)


def packed_rows(slots):
    return HALF if slots == SLOTS else TILE


def dot_nn(a, b):
    return lax.dot_general(a, b, (((1,), (0,)), ((), ())), preferred_element_type=F32)


def dot_nt(a, b):
    return lax.dot_general(a, b, (((1,), (1,)), ((), ())), preferred_element_type=F32)


def cols_before(n, s):
    return (n // TILE) * STRIPS + jnp.clip(n % TILE - STRIPS * s, 0, STRIPS)


def column_facts(virt, s, shape):
    w = iota(shape, 1)
    d = w + 77 * div11(w) + STRIPS * s
    block = d >> 6
    before = [cols_before(BLOCK_WIDTH * b, s) for b in range(BLOCKS + 1)]
    labels = [virt[b] for b in range(BLOCKS)]
    label = jnp.zeros(shape, I32)
    rank = w
    for b in range(BLOCKS):
        base = -before[b]
        for e in range(b):
            base = base + jnp.where(labels[e] == labels[b], before[e + 1] - before[e], 0)
        here = block == b
        label = jnp.where(here, labels[b], label)
        rank = jnp.where(here, w + base, rank)
    return d, block, label, rank


def row_label(virt, block, first):
    label = virt[first]
    for k in (1, 2):
        label = jnp.where(block == first + k, virt[jnp.minimum(first + k, BLOCKS - 1)], label)
    return label


def pack_tiles(slots, virt, pair, aux, pat, a_ref, b_ref, d_ref, packed, send_a, send_b):
    r, s, o = coords()
    first = (STRIPS * r) >> 3
    d, block, label, rank = column_facts(virt, s, (1, WIDE))
    sel = jnp.where((iota((128, WIDE), 0) & (slots - 1)) == rank, 1.0, 0.0).astype(BF16)
    left = iota((HALF, 128), 1) < SLOTS

    def pack(src, count, keep, base):
        n = count * STRIPS
        lines = [src[pl.ds(k, n, stride=STRIPS), :] for k in range(STRIPS)]
        for v in range(8):
            start = WIDE * v
            low, off = start // 128, start % 128
            last = (start + WIDE - 1) // 128
            tile = jnp.concatenate(lines[low : last + 1], axis=1)[:, off : off + WIDE]
            hi, lo = split(jnp.where(keep, tile, 0.0))
            d_ref[pl.ds(v, n, stride=8), :] = dot_nt(hi, sel) + dot_nt(lo, sel)
        d_ref[n * 8 : n * 8 + 8, :] = jnp.zeros((8, 128), F32)
        for k in range(count):
            if slots == SLOTS:
                top = d_ref[pl.ds(TILE * k, HALF), :]
                bottom = d_ref[pl.ds(TILE * k + HALF, HALF), :]
                packed[base + k] = jnp.where(left, top, bottom)
            else:
                packed[base + k] = d_ref[pl.ds(TILE * k, TILE), :]

    row = iota((2 * STRIPS, 1), 0)
    p = jnp.where(row >= STRIPS, 1, 0)
    row_block = (STRIPS * r + row - STRIPS * p) >> 3
    keep = label == (row_label(virt, row_block, first) ^ jnp.where(p == 1, pair[1], pair[0]))
    pack(a_ref, 2, keep, 8)
    send_a()

    screens = []
    for k in range(3):
        x = jnp.minimum(first + k, BLOCKS - 1)
        flag = jnp.zeros((1, WIDE), I32)
        for b in range(BLOCKS):
            flag = jnp.where(block == b, pat[x, b] * pat[b, x], flag)
        screens.append(flag)
    row = iota((TILE, 1), 0)
    q = div11(row)
    row_block = (STRIPS * r + row - STRIPS * q) >> 3
    aux_row = jnp.zeros((TILE, 1), I32)
    for k in range(8):
        aux_row = jnp.where(q == k, aux[8 * o + k], aux_row)
    screen = jnp.where(
        row_block == first, screens[0], jnp.where(row_block == first + 1, screens[1], screens[2])
    )
    target = row_label(virt, row_block, first) ^ aux_row
    pack(b_ref, 8, jnp.logical_and(label == target, screen > 0), 0)
    send_b()


def gather_kernel(
    slots, virt, pair, aux, pat, a_ref, b_ref, aa_ref, sa_ref, d_ref, packed, send, recv, near
):
    r, s, o = coords()
    c, x, y = r % 2, (r // 2) % 4, r // 8

    def at(cc, xx, yy, ss):
        return (yy * 8 + xx * 2 + cc, ss, o)

    zs = {k: at(c, x, y, (s + k) % 8) for k in range(1, 8)}
    planes = {
        (e, k): at(c, (x + k) % 4, (y + e) % 2, s) for e in range(2) for k in range(4) if e + k
    }
    sibling = at(1 - c, x, y, s)
    barrier = pltpu.get_barrier_semaphore()
    for peer in [*zs.values(), *planes.values(), sibling]:
        pl.semaphore_signal(barrier, inc=1, device_id=peer, device_id_type=MESH)

    kinds = {}
    copies = []

    def number(kind):
        return kinds.setdefault(kind, len(kinds))

    def describe(src, dst, peer, kind):
        n = number(kind)
        return pltpu.make_async_remote_copy(
            src_ref=src,
            dst_ref=dst,
            send_sem=send.at[n],
            recv_sem=recv.at[n],
            device_id=peer,
            device_id_type=MESH,
        )

    def put(src, dst, peer, *kind):
        copies.append(describe(src, dst, peer, kind))
        copies[-1].start()

    def arrived(ref, *kind):
        describe(ref, ref, sibling, kind).wait_recv()

    def share(ref, *kind):
        put(ref, ref, sibling, "core", *kind)

    def sign(way, k):
        return k if way else -k

    def a_block(k, ch, cc=c):
        return aa_ref.at[cc, 2 * ch : 2 * ch + 2, :, (s + k + 8) % 8]

    def s_block(k, e, cc=c):
        return sa_ref.at[cc, (x + k + 4) % 4, (y + e) % 2]

    def send_a():
        pl.semaphore_wait(barrier, 15)
        for (e, k), peer in planes.items():
            put(packed.at[8 + (y + e) % 2], aa_ref.at[c, x, y, s], peer, "ax", e, k)
        own = pltpu.make_async_copy(packed.at[8 + y], aa_ref.at[c, x, y, s], near.at[0])
        own.start()
        own.wait()

    def send_b():
        for k in (4, 3, 5, 2, 6, 1, 7):
            put(packed.at[(s + k) % 8], sa_ref.at[c, x, y, s], zs[k], "sz", k)
        own = pltpu.make_async_copy(packed.at[s], sa_ref.at[c, x, y, s], near.at[1])
        own.start()
        own.wait()

    pack_tiles(slots, virt, pair, aux, pat, a_ref, b_ref, d_ref, packed, send_a, send_b)

    def a_ring(h):
        for ch in range(2):
            for way in range(2):
                if h:
                    block = a_block(sign(1 - way, h), ch)
                    if h < 4 or ch != way:
                        arrived(block, "az", way, h - 1, ch)
                        share(block, "az", way, h - 1, ch)
                else:
                    block = a_block(0, ch)
                    if way == 0:
                        share(block, "own", ch)
                if h < 3 or (h == 3 and ch != way):
                    put(block, block, zs[1 if way else 7], "az", way, h, ch)

    def s_arrival(e):
        for way in range(2):
            block = s_block(sign(1 - way, 1), e)
            arrived(block, "sx", way, e)
            if e != way:
                put(block, block, planes[0, 1 if way else 3], "sxx", way)
            share(block, "sx", way, e)

    for e, k in planes:
        arrived(aa_ref.at[c, (x - k + 4) % 4, (y + e) % 2, s], "ax", e, k)
    a_ring(0)
    for k in (1, 7, 2, 6, 3, 5, 4):
        arrived(sa_ref.at[c, x, y, (s - k + 8) % 8], "sz", k)
    put(s_block(0, 0), s_block(0, 0), planes[1, 0], "sy")
    for way in range(2):
        put(s_block(0, 0), s_block(0, 0), planes[0, 1 if way else 3], "sx", way, 0)
    share(s_block(0, 0), "sy", 0)
    a_ring(1)
    arrived(s_block(0, 1), "sy")
    for way in range(2):
        put(s_block(0, 1), s_block(0, 1), planes[0, 1 if way else 3], "sx", way, 1)
    share(s_block(0, 1), "sy", 1)
    s_arrival(0)
    a_ring(2)
    s_arrival(1)
    a_ring(3)
    for way in range(2):
        block = s_block(2, 1 - way)
        arrived(block, "sxx", way)
        share(block, "sxx", way)
    a_ring(4)
    for ch in range(2):
        arrived(a_block(0, ch, 1 - c), "core", "own", ch)
        for way in range(2):
            for h in range(4):
                if h < 3 or ch != way:
                    arrived(a_block(sign(1 - way, h + 1), ch, 1 - c), "core", "az", way, h, ch)
    for e in range(2):
        arrived(s_block(0, e, 1 - c), "core", "sy", e)
        for way in range(2):
            arrived(s_block(sign(1 - way, 1), e, 1 - c), "core", "sx", way, e)
    for way in range(2):
        arrived(s_block(2, 1 - way, 1 - c), "core", "sxx", way)
    for copy in copies:
        copy.wait_send()


def product_kernel(
    slots, virt, pair, aux, aa_ref, sa_ref, z_ref, a2, s2, v1, v2, zs, whi, wlo, lists, counts
):
    r, s, o = coords()
    nat, per_label = 8 * slots, slots // 8
    core, x_me, pair_me = r % 2, (r // 2) % 4, r // 8
    h = aux[8 * o + s]
    hp = h ^ pair[pair_me]
    left = iota((HALF, 128), 1) < SLOTS

    def unpack(k, _):
        c, x, y = k % 2, (k // 2) % 4, k // 8
        base = pl.multiple_of(k * TILE, 8)
        for src, dst in ((sa_ref, s2), (aa_ref, a2)):
            if slots != SLOTS:
                for j in range(8):
                    dst[pl.ds(base, TILE), pl.ds(128 * j, 128)] = src[c, x, y, j]
                continue
            for j in range(4):
                even, odd = src[c, x, y, 2 * j], src[c, x, y, 2 * j + 1]
                top = jnp.where(left, even, pltpu.roll(odd, SLOTS, 1))
                bottom = jnp.where(left, pltpu.roll(even, SLOTS, 1), odd)
                dst[pl.ds(base, HALF), pl.ds(128 * j, 128)] = top
                dst[pl.ds(base + HALF, TILE - HALF), pl.ds(128 * j, 128)] = bottom[: TILE - HALF]
        return 0

    lax.fori_loop(0, ROWS, unpack, 0)
    for ref in (s2, a2):
        ref[VIRTUALS:, :] = jnp.zeros((BLOCK_WIDTH, nat), F32)

    for g in range(LABELS):
        counts[g] = 0
        for j in range(per_label):
            lists[per_label * g + j] = BLOCKS
    places = []
    for b in range(BLOCKS):
        g = virt[b]
        n = counts[g]
        lists[per_label * g + jnp.minimum(n, per_label - 1)] = b
        counts[g] = n + 1
        places.append(n)

    group = iota((8, 1), 0)
    d, block, label, rank = column_facts(virt, group, (8, WIDE))
    place = jnp.zeros((8, WIDE), I32)
    for b in range(BLOCKS):
        place = jnp.where(block == b, places[b], place)
    natural = place * BLOCK_WIDTH + (d & (BLOCK_WIDTH - 1))

    tiles = (2 * x_me + core, 8 + 2 * x_me + core)
    bases = [pl.multiple_of(t * TILE, 8) for t in tiles]
    firsts = [(STRIPS * t) >> 3 for t in tiles]
    row = iota((TILE, 1), 0)
    row_blocks = [(t * TILE + row) >> 6 for t in tiles]
    labels = jnp.concatenate([row_label(virt, b, f) for b, f in zip(row_blocks, firsts)], axis=0)

    def to_natural(x, target):
        hi, lo = split(x)
        both = jnp.concatenate([hi, lo], axis=0)
        target = jnp.concatenate([target, target], axis=0)
        total = jnp.zeros((2 * WIDE, nat), F32)
        for k in range(8):
            j, shift = (slots * k) // 128, (slots * k) % 128
            spread = jnp.where(iota((128, WIDE), 0) == rank[k : k + 1] + shift, 1.0, 0.0)
            spread = spread.astype(BF16)
            dense = dot_nn(both[:, 128 * j : 128 * j + 128], spread)
            dense = jnp.where(label[k : k + 1] == target, dense, 0.0).astype(BF16)
            pick = jnp.where(iota((nat, WIDE), 0) == natural[k : k + 1], 1.0, 0.0).astype(BF16)
            total = total + dot_nt(dense, pick)
        return total[:WIDE] + total[WIDE:]

    own = [s2[pl.ds(b, TILE), :] for b in bases]
    own_natural = to_natural(jnp.concatenate(own, axis=0), labels ^ h)

    def load_rows(src, g, half):
        for j in range(4):
            b = lists[per_label * g + 4 * half + j]
            hi, lo = split(src[pl.ds(pl.multiple_of(b * BLOCK_WIDTH, BLOCK_WIDTH), BLOCK_WIDTH), :])
            whi[pl.ds(BLOCK_WIDTH * j, BLOCK_WIDTH), :] = hi
            wlo[pl.ds(BLOCK_WIDTH * j, BLOCK_WIDTH), :] = lo

    def dot3(dot, a):
        hi, lo = split(a)
        return dot(hi, whi[...]) + dot(lo, whi[...]) + dot(hi, wlo[...])

    v1[...] = jnp.zeros_like(v1)
    v2[...] = jnp.zeros_like(v2)
    zs[...] = jnp.zeros_like(zs)
    for t in range(2):
        last = (STRIPS * tiles[t] + STRIPS - 1) >> 3

        def first_product(x, _, t=t):
            g1 = virt[x] ^ h
            g2 = virt[x] ^ hp
            here = row_blocks[t] == x
            mine = jnp.where(here, own[t], 0.0)
            mine_natural = jnp.where(here, own_natural[TILE * t : TILE * t + TILE], 0.0)
            for half in range(nat // 256):
                part = slice(256 * half, 256 * half + 256)

                @pl.when(counts[g1] > 4 * half)
                def _():
                    load_rows(a2, g1, half)
                    v2[t] += dot3(dot_nn, mine_natural[:, part])

                @pl.when(counts[g2] > 4 * half)
                def _():
                    load_rows(a2, g2, half)
                    v1[t, :, part] += dot3(dot_nt, mine)

            return 0

        lax.fori_loop(firsts[t], last + 1, first_product, 0)

    turned = to_natural(jnp.concatenate([v2[0], v2[1]], axis=0), labels ^ hp)
    for t in range(2):
        last = (STRIPS * tiles[t] + STRIPS - 1) >> 3
        y = turned[TILE * t : TILE * t + TILE] - v1[t]

        def second_product(x, _, t=t, y=y):
            g2 = virt[x] ^ hp
            mine = jnp.where(row_blocks[t] == x, y, 0.0)
            for half in range(nat // 256):

                @pl.when(counts[g2] > 4 * half)
                def _():
                    load_rows(s2, g2, half)
                    zs[t, :TILE] += dot3(dot_nn, mine[:, 256 * half : 256 * half + 256])

            return 0

        lax.fori_loop(firsts[t], last + 1, second_product, 0)

    for t in range(2):
        for k in range(8):
            if slots != SLOTS:
                z_ref[t, k] = zs[t, :TILE, pl.ds(128 * k, 128)]
                continue
            j = k // 2
            top = zs[t, 0:HALF, pl.ds(128 * j, 128)]
            bottom = zs[t, HALF : 2 * HALF, pl.ds(128 * j, 128)]
            if k % 2 == 0:
                z_ref[t, k] = jnp.where(left, top, pltpu.roll(bottom, SLOTS, 1))
            else:
                z_ref[t, k] = jnp.where(left, pltpu.roll(top, SLOTS, 1), bottom)


def scatter_kernel(slots, virt, pair, z_ref, out_ref, parts, low_ref, high_ref, send, recv, near):
    r, s, o = coords()
    y, rest = r // 8, r % 8
    alone = jnp.where(y == o, 1, 0)
    barrier = pltpu.get_barrier_semaphore()

    def greet(e, k):
        pl.semaphore_signal(
            barrier, inc=1, device_id=(o * 8 + rest, (s + k) % 8, e), device_id_type=MESH
        )

    def describe(e, k):
        return pltpu.make_async_remote_copy(
            src_ref=z_ref.at[e, (s + k) % 8],
            dst_ref=parts.at[o, s],
            send_sem=send.at[8 * e + k],
            recv_sem=recv.at[8 * o + k],
            device_id=(e * 8 + rest, (s + k) % 8, y),
            device_id_type=MESH,
        )

    def sender(e, k):
        describe(e, k).start()

    def receive(e, k):
        spot = parts.at[e, (s - k + 8) % 8]
        pltpu.make_async_remote_copy(
            src_ref=spot,
            dst_ref=spot,
            send_sem=send.at[0],
            recv_sem=recv.at[8 * e + k],
            device_id=(o * 8 + rest, (s + 1) % 8, e),
            device_id_type=MESH,
        ).wait_recv()

    def finish(e, k):
        describe(e, k).wait_send()

    def each(fn, mine):
        for k in (4, 3, 5, 2, 6, 1, 7, 0):
            for e in range(2):
                if k:
                    fn(e, k)
                else:
                    pl.when(jnp.logical_or(y != o, mine != e))(functools.partial(fn, e, k))

    each(greet, o)
    pl.semaphore_wait(barrier, 16 - alone)
    each(sender, y)

    @pl.when(y == o)
    def _():
        copy = pltpu.make_async_copy(z_ref.at[y, s], parts.at[o, s], near.at[0])
        copy.start()
        copy.wait()

    first = (STRIPS * r) >> 3
    d, block, label, rank = column_facts(virt, s, (1, WIDE))
    each(receive, o)
    total = parts[0, 0]
    for k in range(1, 16):
        total = total + parts[k // 8, k % 8]
    hi, lo = split(0.5 * total)
    rows = packed_rows(slots)
    row = iota((rows, 1), 0)
    for half in range(128 // slots):
        spread = jnp.where(iota((128, WIDE), 0) == rank + slots * half, 1.0, 0.0).astype(BF16)
        dense = dot_nn(hi, spread) + dot_nn(lo, spread)
        row_block = (TILE * r + rows * half + row) >> 6
        keep = label == (row_label(virt, row_block, first) ^ pair[o])
        dense = jnp.where(keep, dense, 0.0)
        low_ref[rows * half : rows * half + rows, :] = dense[:, :128]
        high_ref[rows * half : rows * half + rows, :] = jnp.concatenate(
            [dense[:, 128:], jnp.zeros((rows, 256 - WIDE), F32)], axis=1
        )
    lines = []
    for v in range(8):
        low, high = low_ref[pl.ds(v, STRIPS, stride=8), :], high_ref[pl.ds(v, STRIPS, stride=8), :]
        lines.append(jnp.concatenate([low, high[:, : WIDE - 128]], axis=1))
    for k in range(STRIPS):
        v, w = (128 * k) // WIDE, (128 * k) % WIDE
        piece = lines[v][:, w : min(WIDE, w + 128)]
        if w + 128 > WIDE:
            piece = jnp.concatenate([piece, lines[v + 1][:, : w + 128 - WIDE]], axis=1)
        out_ref[pl.ds(k, STRIPS, stride=STRIPS), :] = piece
    each(finish, y)


def smem(n):
    return [pl.BlockSpec(memory_space=pltpu.SMEM)] * n


def vmem(n):
    return [pl.BlockSpec(memory_space=pltpu.VMEM)] * n


def shape(*dims):
    return jax.ShapeDtypeStruct(dims, F32)


def run_gather(slots, virt, pair, aux, pat, a, b):
    rows = packed_rows(slots)
    full = shape(2, 4, 2, 8, rows, 128)
    return pl.pallas_call(
        functools.partial(gather_kernel, slots),
        out_shape=(full, full),
        in_specs=smem(4) + vmem(2),
        out_specs=tuple(vmem(2)),
        scratch_shapes=[
            pltpu.VMEM((8 * TILE + 8, 128), F32),
            pltpu.VMEM((10, rows, 128), F32),
            pltpu.SemaphoreType.DMA((64,)),
            pltpu.SemaphoreType.DMA((64,)),
            pltpu.SemaphoreType.DMA((2,)),
        ],
        compiler_params=pltpu.CompilerParams(
            collective_id=0 if slots == SLOTS else 2, has_side_effects=True, vmem_limit_bytes=32 * MIB
        ),
    )(virt, pair, aux, pat, a, b)


def run_product(slots, virt, pair, aux, aa, sa):
    nat = 8 * slots
    tall = pltpu.VMEM((VIRTUALS + BLOCK_WIDTH, nat), F32)
    return pl.pallas_call(
        functools.partial(product_kernel, slots),
        out_shape=shape(2, 8, packed_rows(slots), 128),
        in_specs=smem(3) + vmem(2),
        out_specs=vmem(1)[0],
        scratch_shapes=[
            tall,
            tall,
            pltpu.VMEM((2, TILE, nat), F32),
            pltpu.VMEM((2, TILE, nat), F32),
            pltpu.VMEM((2, 2 * HALF, nat), F32),
            pltpu.VMEM((256, nat), BF16),
            pltpu.VMEM((256, nat), BF16),
            pltpu.SMEM((slots,), I32),
            pltpu.SMEM((8,), I32),
        ],
        compiler_params=pltpu.CompilerParams(vmem_limit_bytes=48 * MIB),
    )(virt, pair, aux, aa, sa)


def run_scatter(slots, virt, pair, z):
    return pl.pallas_call(
        functools.partial(scatter_kernel, slots),
        out_shape=shape(121, 128),
        in_specs=smem(2) + vmem(1),
        out_specs=vmem(1)[0],
        scratch_shapes=[
            pltpu.VMEM((2, 8, packed_rows(slots), 128), F32),
            pltpu.VMEM((2 * HALF, 128), F32),
            pltpu.VMEM((2 * HALF, 128), F32),
            pltpu.SemaphoreType.DMA((16,)),
            pltpu.SemaphoreType.DMA((16,)),
            pltpu.SemaphoreType.DMA((1,)),
        ],
        compiler_params=pltpu.CompilerParams(
            collective_id=1 if slots == SLOTS else 3, has_side_effects=True, vmem_limit_bytes=32 * MIB
        ),
    )(virt, pair, z)


def packed_path(slots, amplitudes, aux_factor, virt, pair, aux, pat):
    aa, sa = run_gather(
        slots, virt, pair, aux, pat, amplitudes.reshape(242, 128), aux_factor.reshape(968, 128)
    )
    z = run_product(slots, virt, pair, aux, aa, sa)
    return run_scatter(slots, virt, pair, z).reshape(1, 1, 1, TILE * WIDE)


def widest_label(virt):
    edges = np.arange(BLOCKS + 1)[:, None] * BLOCK_WIDTH
    before = edges // TILE * STRIPS + np.clip(edges % TILE - STRIPS * np.arange(COLS), 0, STRIPS)
    share = jnp.asarray(before[1:] - before[:-1], I32)
    same = virt[:, None] == jnp.arange(LABELS, dtype=I32)
    totals = jnp.sum(jnp.where(same[:, :, None], share[:, None, :], 0), axis=0)
    return jnp.max(totals)


def block_onehot(indices, block_count):
    return indices[..., None] // BLOCK_WIDTH == jnp.arange(block_count, dtype=jnp.int32)


def label_lookup(hot_table, virt_irrep):
    return jnp.sum(jnp.where(hot_table, virt_irrep, 0), axis=-1)


def dense_path(amplitudes, aux_factor, virt_irrep, pair_irrep, aux_irrep, block_pattern):
    tile_count = lax.axis_size("row")
    col_count = lax.axis_size("col")
    local_rows = VIRTUALS // tile_count
    sub_width = local_rows // col_count
    amplitudes = amplitudes.reshape(amplitudes.shape[0], local_rows, tile_count, sub_width)
    aux_factor = aux_factor.reshape(aux_factor.shape[0], local_rows, tile_count, sub_width)
    block_count = virt_irrep.shape[0]
    row_index = lax.axis_index("row") * local_rows + jnp.arange(local_rows, dtype=jnp.int32)
    col_index = (
        jnp.arange(tile_count, dtype=jnp.int32)[:, None] * local_rows
        + lax.axis_index("col") * sub_width
        + jnp.arange(sub_width, dtype=jnp.int32)[None, :]
    )
    row_hot = block_onehot(row_index, block_count)
    col_hot = block_onehot(col_index, block_count)
    product = jnp.bitwise_xor(
        label_lookup(row_hot, virt_irrep)[:, None, None], label_lookup(col_hot, virt_irrep)[None]
    )
    kept_mask = product[None] == pair_irrep[:, None, None, None]
    masked = jnp.where(kept_mask, amplitudes, 0.0)
    pattern = (block_pattern * block_pattern.T).astype(jnp.float32)
    screen = (
        jnp.einsum(
            "ak,kl,itl->ait", row_hot.astype(jnp.float32), pattern, col_hot.astype(jnp.float32)
        )
        > 0.5
    )
    aux_here = aux_factor.shape[0]
    aux_labels = lax.dynamic_slice_in_dim(aux_irrep, lax.axis_index("occ") * aux_here, aux_here, 0)
    aux_mask = jnp.logical_and(screen[None], product[None] == aux_labels[:, None, None, None])
    factor = jnp.where(aux_mask, aux_factor, 0.0)
    half_pairs = masked.shape[0] // lax.axis_size("occ")
    masked = lax.dynamic_slice_in_dim(masked, lax.axis_index("occ") * half_pairs, half_pairs, 0)
    factor = lax.all_gather(factor, "occ", axis=0, tiled=True)
    pair_count = masked.shape[0]
    aux_count = factor.shape[0]
    split_view = masked.reshape(pair_count, col_count, sub_width, tile_count, sub_width)
    swapped = lax.all_to_all(
        lax.all_to_all(split_view, "row", split_axis=3, concat_axis=3, tiled=True),
        "col",
        split_axis=1,
        concat_axis=4,
        tiled=True,
    )
    mirrored = swapped.reshape(pair_count, sub_width, tile_count, local_rows).transpose(0, 3, 2, 1)
    antisym = masked - mirrored
    columns = lax.all_gather(factor, "row", axis=1, tiled=True)
    columns = columns.reshape(aux_count, tile_count, local_rows, tile_count * sub_width)
    rows_panel = lax.all_gather(factor, "col", axis=3, tiled=True).reshape(
        aux_count, local_rows, tile_count * local_rows
    )
    chosen = columns
    contracted = jnp.einsum(
        "pcik,qikn->qpcn",
        lax.all_gather(antisym, "col", axis=3, tiled=True),
        chosen,
        precision=lax.Precision.HIGHEST,
    )
    chosen = rows_panel
    summed = lax.psum_scatter(
        jnp.einsum("qca,qpcn->apn", chosen, contracted, precision=lax.Precision.HIGHEST),
        "row",
        scatter_dimension=0,
        tiled=True,
    )
    pairs_out = summed.shape[1]
    result = (
        (0.5 * summed).reshape(local_rows, pairs_out, tile_count, sub_width).transpose(1, 0, 2, 3)
    )
    return result.reshape(pairs_out, 1, 1, local_rows * tile_count * sub_width)


def per_device(*args):
    widest = widest_label(args[2])
    paths = [functools.partial(packed_path, SLOTS), functools.partial(packed_path, 128), dense_path]
    which = jnp.where(widest > SLOTS, 1, 0) + jnp.where(widest > 128, 1, 0)
    return lax.switch(which, paths, *args)


def solution(mesh):
    placed = (P(None, "row", "col", None), P("occ", "row", "col", None), P(), P(), P(), P())
    return jax.shard_map(
        per_device,
        mesh=mesh,
        in_specs=placed,
        out_specs=P("occ", "row", "col", None),
        check_vma=False,
    )
```

```python
import functools

import jax
import jax.numpy as jnp
from jax import lax
from jax.experimental import pallas as pl
from jax.experimental.pallas import tpu as pltpu
from jax.sharding import PartitionSpec as P

VIRTUALS = 1408
BLOCK_WIDTH = 64
BLOCKS = 22
LABELS = 8
ROWS, COLS = 16, 8
TILE = 88
WIDE = 176
STRIPS = 11
SLOTS = 64
HALF = 48
MESH = pl.DeviceIdType.MESH
MIB = 1 << 20
F32, BF16, I32 = jnp.float32, jnp.bfloat16, jnp.int32


def coords():
    return lax.axis_index("row"), lax.axis_index("col"), lax.axis_index("occ")


def iota(shape, dim):
    return lax.broadcasted_iota(I32, shape, dim)


def div11(v):
    return (v * 5958) >> 16


def split(x):
    hi = x.astype(BF16)
    return hi, (x - hi.astype(F32)).astype(BF16)


def packed_rows(slots):
    return HALF if slots == SLOTS else TILE


def dot_nn(a, b):
    return lax.dot_general(a, b, (((1,), (0,)), ((), ())), preferred_element_type=F32)


def dot_nt(a, b):
    return lax.dot_general(a, b, (((1,), (1,)), ((), ())), preferred_element_type=F32)


def cols_before(n, s):
    return (n // TILE) * STRIPS + jnp.clip(n % TILE - STRIPS * s, 0, STRIPS)


def column_facts(virt, s, shape):
    w = iota(shape, 1)
    d = w + 77 * div11(w) + STRIPS * s
    block = d >> 6
    before = [cols_before(BLOCK_WIDTH * b, s) for b in range(BLOCKS + 1)]
    labels = [virt[b] for b in range(BLOCKS)]
    label = jnp.zeros(shape, I32)
    rank = w
    for b in range(BLOCKS):
        base = -before[b]
        for e in range(b):
            base = base + jnp.where(labels[e] == labels[b], before[e + 1] - before[e], 0)
        here = block == b
        label = jnp.where(here, labels[b], label)
        rank = jnp.where(here, w + base, rank)
    return d, block, label, rank


def row_label(virt, block, first):
    label = virt[first]
    for k in (1, 2):
        label = jnp.where(block == first + k, virt[jnp.minimum(first + k, BLOCKS - 1)], label)
    return label


def pack_tiles(slots, virt, pair, aux, pat, a_ref, b_ref, d_ref, packed, send_a, send_b):
    r, s, o = coords()
    first = (STRIPS * r) >> 3
    d, block, label, rank = column_facts(virt, s, (1, WIDE))
    sel = jnp.where((iota((128, WIDE), 0) & (slots - 1)) == rank, 1.0, 0.0).astype(BF16)
    left = iota((HALF, 128), 1) < SLOTS

    def pack(src, count, keep, base):
        n = count * STRIPS
        if len(src.shape) == 3:
            lines = [src[pl.ds(k, n, stride=STRIPS), 0, :] for k in range(STRIPS)]
        else:
            lines = [src[pl.ds(k, n, stride=STRIPS), :] for k in range(STRIPS)]
        for v in range(8):
            start = WIDE * v
            low, off = start // 128, start % 128
            last = (start + WIDE - 1) // 128
            tile = jnp.concatenate(lines[low : last + 1], axis=1)[:, off : off + WIDE]
            hi, lo = split(jnp.where(keep, tile, 0.0))
            d_ref[pl.ds(v, n, stride=8), :] = dot_nt(hi, sel) + dot_nt(lo, sel)
        d_ref[n * 8 : n * 8 + 8, :] = jnp.zeros((8, 128), F32)
        for k in range(count):
            if slots == SLOTS:
                top = d_ref[pl.ds(TILE * k, HALF), :]
                bottom = d_ref[pl.ds(TILE * k + HALF, HALF), :]
                packed[base + k] = jnp.where(left, top, bottom)
            else:
                packed[base + k] = d_ref[pl.ds(TILE * k, TILE), :]

    row = iota((2 * STRIPS, 1), 0)
    p = jnp.where(row >= STRIPS, 1, 0)
    row_block = (STRIPS * r + row - STRIPS * p) >> 3
    keep = label == (row_label(virt, row_block, first) ^ jnp.where(p == 1, pair[1], pair[0]))
    pack(a_ref, 2, keep, 8)
    send_a()

    screens = []
    for k in range(3):
        x = jnp.minimum(first + k, BLOCKS - 1)
        flag = jnp.zeros((1, WIDE), I32)
        for b in range(BLOCKS):
            flag = jnp.where(block == b, pat[x, b] * pat[b, x], flag)
        screens.append(flag)
    row = iota((TILE, 1), 0)
    q = div11(row)
    row_block = (STRIPS * r + row - STRIPS * q) >> 3
    aux_row = jnp.zeros((TILE, 1), I32)
    for k in range(8):
        aux_row = jnp.where(q == k, aux[8 * o + k], aux_row)
    screen = jnp.where(
        row_block == first, screens[0], jnp.where(row_block == first + 1, screens[1], screens[2])
    )
    target = row_label(virt, row_block, first) ^ aux_row
    pack(b_ref, 8, jnp.logical_and(label == target, screen > 0), 0)
    send_b()


def to_natural(slots, x, target, label, spread, pick):
    hi, lo = split(x)
    both = jnp.concatenate([hi, lo], axis=0)
    target = jnp.concatenate([target, target], axis=0)
    total = jnp.zeros((both.shape[0], 8 * slots), F32)
    for k in range(8):
        j = (slots * k) // 128
        dense = dot_nn(both[:, 128 * j : 128 * j + 128], spread[k])
        dense = jnp.where(label[k : k + 1] == target, dense, 0.0).astype(BF16)
        total = total + dot_nt(dense, pick[k])
    return total[: x.shape[0]] + total[x.shape[0] :]


def my_tiles(r):
    tiles = (r % 8, 8 + r % 8)
    bases = [pl.multiple_of(t * TILE, 8) for t in tiles]
    firsts = [(STRIPS * t) >> 3 for t in tiles]
    row_blocks = [(t * TILE + iota((TILE, 1), 0)) >> 6 for t in tiles]
    return tiles, bases, firsts, row_blocks


def tile_labels(virt, firsts, row_blocks):
    return jnp.concatenate([row_label(virt, b, f) for b, f in zip(row_blocks, firsts)], axis=0)


def gather_kernel(
    slots,
    virt,
    pair,
    aux,
    pat,
    a_ref,
    b_ref,
    a2,
    s2,
    own_natural,
    label_ref,
    spread_ref,
    pick_ref,
    aa_ref,
    sa_ref,
    a_lines,
    d_ref,
    packed,
    send,
    recv,
    near,
):
    r, s, o = coords()
    c, x, y = r % 2, (r // 2) % 4, r // 8

    def at(cc, xx, yy, ss):
        return (yy * 8 + xx * 2 + cc, ss, o)

    zs = {k: at(c, x, y, (s + k) % 8) for k in range(1, 8)}
    planes = {
        (e, k): at(c, (x + k) % 4, (y + e) % 2, s) for e in range(2) for k in range(4) if e + k
    }
    sibling = at(1 - c, x, y, s)
    barrier = pltpu.get_barrier_semaphore()
    for peer in [*zs.values(), *planes.values(), sibling]:
        pl.semaphore_signal(barrier, inc=1, device_id=peer, device_id_type=MESH)

    kinds = {}
    copies = []

    def number(kind):
        return kinds.setdefault(kind, len(kinds))

    def describe(src, dst, peer, kind):
        n = number(kind)
        return pltpu.make_async_remote_copy(
            src_ref=src,
            dst_ref=dst,
            send_sem=send.at[n],
            recv_sem=recv.at[n],
            device_id=peer,
            device_id_type=MESH,
        )

    def put(src, dst, peer, *kind):
        copies.append(describe(src, dst, peer, kind))
        copies[-1].start()

    def arrived(ref, *kind):
        describe(ref, ref, sibling, kind).wait_recv()

    def share(ref, *kind):
        put(ref, ref, sibling, "core", *kind)

    def sign(way, k):
        return k if way else -k

    def a_block(k, ch, cc=c):
        return aa_ref.at[cc, 2 * ch : 2 * ch + 2, :, (s + k + 8) % 8]

    def s_block(k, e, cc=c):
        return sa_ref.at[cc, (x + k + 4) % 4, (y + e) % 2]

    def send_a():
        pl.semaphore_wait(barrier, 15)
        for (e, k), peer in planes.items():
            put(packed.at[8 + (y + e) % 2], aa_ref.at[c, x, y, s], peer, "ax", e, k)
        own = pltpu.make_async_copy(packed.at[8 + y], aa_ref.at[c, x, y, s], near.at[0])
        own.start()
        own.wait()

    def send_b():
        for k in (4, 3, 5, 2, 6, 1, 7):
            put(packed.at[(s + k) % 8], sa_ref.at[c, x, y, s], zs[k], "sz", k)
        own = pltpu.make_async_copy(packed.at[s], sa_ref.at[c, x, y, s], near.at[1])
        own.start()
        own.wait()

    amplitudes = pltpu.make_async_copy(a_ref, a_lines, near.at[2])
    amplitudes.start()
    amplitudes.wait()
    pack_tiles(slots, virt, pair, aux, pat, a_lines, b_ref, d_ref, packed, send_a, send_b)

    def tile_base(xx, yy, cc):
        return pl.multiple_of((yy * 8 + xx * 2 + cc) * TILE, 8)

    half_lanes = iota((HALF, 128), 1) < SLOTS

    def take_a(k, ch, cc=c):
        ss = (s + k + 8) % 8
        lane = pl.multiple_of(128 * (ss // (128 // slots)), 128)

        def take(n, _):
            xx, yy = 2 * ch + n // 2, n % 2
            base = tile_base(xx, yy, cc)
            piece = aa_ref[cc, xx, yy, ss]
            if slots != SLOTS:
                a2[pl.ds(base, TILE), pl.ds(lane, 128)] = piece
                return 0
            odd = ss % 2 == 1
            turned = pltpu.roll(piece, SLOTS, 1)
            top = jnp.where(odd, turned, piece)
            bottom = jnp.where(odd, piece, turned)
            mine = jnp.logical_xor(half_lanes, odd)
            for at_row, value, n_rows in ((base, top, HALF), (base + HALF, bottom, TILE - HALF)):
                rows = pl.ds(pl.multiple_of(at_row, 8), n_rows)
                there = a2[rows, pl.ds(lane, 128)]
                a2[rows, pl.ds(lane, 128)] = jnp.where(mine[:n_rows], value[:n_rows], there)
            return 0

        lax.fori_loop(0, 4, take, 0)

    def take_s(k, e, cc=c):
        xx, yy = (x + k + 4) % 4, (y + e) % 2
        base = tile_base(xx, yy, cc)
        if slots != SLOTS:
            for j in range(8):
                s2[pl.ds(base, TILE), pl.ds(128 * j, 128)] = sa_ref[cc, xx, yy, j]
            return
        for j in range(4):
            even, odd = sa_ref[cc, xx, yy, 2 * j], sa_ref[cc, xx, yy, 2 * j + 1]
            top = jnp.where(half_lanes, even, pltpu.roll(odd, SLOTS, 1))
            bottom = jnp.where(half_lanes, pltpu.roll(even, SLOTS, 1), odd)
            s2[pl.ds(base, HALF), pl.ds(128 * j, 128)] = top
            s2[pl.ds(base + HALF, TILE - HALF), pl.ds(128 * j, 128)] = bottom[: TILE - HALF]

    def a_ring(h):
        for ch in range(2):
            for way in range(2):
                block = a_block(sign(1 - way, h), ch)
                if h and (h < 4 or ch != way):
                    arrived(block, "az", way, h - 1, ch)
                if h < 3 or (h == 3 and ch != way):
                    put(block, block, zs[1 if way else 7], "az", way, h, ch)
                if h and (h < 4 or ch != way):
                    share(block, "az", way, h - 1, ch)
                if h == 0 and way == 0:
                    share(block, "own", ch)

    def a_take(h):
        for ch in range(2):
            for way in range(2):
                if (h and (h < 4 or ch != way)) or (h == 0 and way == 0):
                    take_a(sign(1 - way, h), ch)

    def a_sibling(h):
        for ch in range(2):
            if h == 0:
                arrived(a_block(0, ch, 1 - c), "core", "own", ch)
                take_a(0, ch, 1 - c)
                continue
            for way in range(2):
                if h < 4 or ch != way:
                    k = sign(1 - way, h)
                    arrived(a_block(k, ch, 1 - c), "core", "az", way, h - 1, ch)
                    take_a(k, ch, 1 - c)

    def s_arrival(e):
        for way in range(2):
            block = s_block(sign(1 - way, 1), e)
            arrived(block, "sx", way, e)
            if e != way:
                put(block, block, planes[0, 1 if way else 3], "sxx", way)
            share(block, "sx", way, e)

    def s_take(e):
        for way in range(2):
            take_s(sign(1 - way, 1), e)

    def s_sibling(e):
        for way in range(2):
            k = sign(1 - way, 1)
            arrived(s_block(k, e, 1 - c), "core", "sx", way, e)
            take_s(k, e, 1 - c)

    def s_start(e):
        block = s_block(0, e)
        for way in range(2):
            put(block, block, planes[0, 1 if way else 3], "sx", way, e)
        share(block, "sy", e)

    def s_start_sibling(e):
        arrived(s_block(0, e, 1 - c), "core", "sy", e)
        take_s(0, e, 1 - c)

    for e, k in planes:
        arrived(aa_ref.at[c, (x - k + 4) % 4, (y + e) % 2, s], "ax", e, k)
    a_ring(0)

    group = iota((8, 1), 0)
    d, block, label, rank = column_facts(virt, group, (8, WIDE))
    place = jnp.zeros((8, WIDE), I32)
    for b in range(BLOCKS):
        seen = 0
        for e in range(b):
            seen = seen + jnp.where(virt[e] == virt[b], 1, 0)
        place = jnp.where(block == b, seen, place)
    natural = place * BLOCK_WIDTH + (d & (BLOCK_WIDTH - 1))
    label_ref[...] = label
    for k in range(8):
        shift = (slots * k) % 128
        spread = jnp.where(iota((128, WIDE), 0) == rank[k : k + 1] + shift, 1.0, 0.0)
        spread_ref[k] = spread.astype(BF16)
    a2[...] = jnp.zeros_like(a2)
    s2[VIRTUALS:, :] = jnp.zeros((BLOCK_WIDTH, 8 * slots), F32)

    def build_picks(ks):
        for k in ks:
            pick = jnp.where(iota((8 * slots, WIDE), 0) == natural[k : k + 1], 1.0, 0.0)
            pick_ref[k] = pick.astype(BF16)

    build_picks(range(4))
    for k in (1, 7, 2, 6, 3, 5, 4):
        arrived(sa_ref.at[c, x, y, (s - k + 8) % 8], "sz", k)
    put(s_block(0, 0), s_block(0, 0), planes[1, 0], "sy")
    s_start(0)
    a_take(0)
    take_s(0, 0)
    build_picks(range(4, 8))
    a_ring(1)
    arrived(s_block(0, 1), "sy")
    s_start(1)
    take_s(0, 1)
    a_take(1)
    s_arrival(0)
    s_start_sibling(0)
    s_start_sibling(1)
    a_ring(2)
    s_take(0)
    a_sibling(0)
    a_sibling(1)
    a_take(2)
    s_arrival(1)
    a_ring(3)
    tiles, bases, firsts, row_blocks = my_tiles(r)
    target = tile_labels(virt, firsts, row_blocks) ^ aux[8 * o + s]
    own = jnp.concatenate([s2[pl.ds(b, TILE), :] for b in bases], axis=0)
    own_natural[...] = to_natural(slots, own, target, label, spread_ref, pick_ref)
    s_take(1)
    a_take(3)
    s_sibling(0)
    a_sibling(2)
    for way in range(2):
        block = s_block(2, 1 - way)
        arrived(block, "sxx", way)
        share(block, "sxx", way)
    a_ring(4)
    s_sibling(1)
    a_sibling(3)
    for way in range(2):
        take_s(2, 1 - way)
    a_take(4)
    for way in range(2):
        arrived(s_block(2, 1 - way, 1 - c), "core", "sxx", way)
        take_s(2, 1 - way, 1 - c)
    a_sibling(4)
    for copy in copies:
        copy.wait_send()


def product_kernel(
    slots,
    virt,
    pair,
    aux,
    a2,
    s2,
    own_natural,
    label_ref,
    spread_ref,
    pick_ref,
    z_ref,
    v1,
    v2,
    zs,
    whi,
    wlo,
    lists,
    counts,
):
    r, s, o = coords()
    nat, per_label = 8 * slots, slots // 8
    h = aux[8 * o + s]
    hp = h ^ pair[r // 8]
    left = iota((HALF, 128), 1) < SLOTS
    for g in range(LABELS):
        counts[g] = 0
        for j in range(per_label):
            lists[per_label * g + j] = BLOCKS
    for b in range(BLOCKS):
        g = virt[b]
        n = counts[g]
        lists[per_label * g + jnp.minimum(n, per_label - 1)] = b
        counts[g] = n + 1
    tiles, bases, firsts, row_blocks = my_tiles(r)
    labels = tile_labels(virt, firsts, row_blocks)

    def load_rows(src, g, half):
        for j in range(4):
            b = lists[per_label * g + 4 * half + j]
            hi, lo = split(src[pl.ds(pl.multiple_of(b * BLOCK_WIDTH, BLOCK_WIDTH), BLOCK_WIDTH), :])
            whi[pl.ds(BLOCK_WIDTH * j, BLOCK_WIDTH), :] = hi
            wlo[pl.ds(BLOCK_WIDTH * j, BLOCK_WIDTH), :] = lo

    def dot3(dot, a):
        hi, lo = split(a)
        return dot(hi, whi[...]) + dot(lo, whi[...]) + dot(hi, wlo[...])

    v1[...] = jnp.zeros_like(v1)
    v2[...] = jnp.zeros_like(v2)
    zs[...] = jnp.zeros_like(zs)
    for t in range(2):
        last = (STRIPS * tiles[t] + STRIPS - 1) >> 3

        def first_product(x, _, t=t):
            g1 = virt[x] ^ h
            g2 = virt[x] ^ hp
            here = row_blocks[t] == x
            mine = jnp.where(here, s2[pl.ds(bases[t], TILE), :], 0.0)
            mine_natural = jnp.where(here, own_natural[TILE * t : TILE * t + TILE, :], 0.0)
            for half in range(nat // 256):
                part = slice(256 * half, 256 * half + 256)

                @pl.when(counts[g1] > 4 * half)
                def _():
                    load_rows(a2, g1, half)
                    v2[t] += dot3(dot_nn, mine_natural[:, part])

                @pl.when(counts[g2] > 4 * half)
                def _():
                    load_rows(a2, g2, half)
                    v1[t, :, part] += dot3(dot_nt, mine)

            return 0

        lax.fori_loop(firsts[t], last + 1, first_product, 0)

    v2_rows = jnp.concatenate([v2[0], v2[1]], axis=0)
    turned = to_natural(slots, v2_rows, labels ^ hp, label_ref[...], spread_ref, pick_ref)
    for t in range(2):
        last = (STRIPS * tiles[t] + STRIPS - 1) >> 3
        y = turned[TILE * t : TILE * t + TILE] - v1[t]

        def second_product(x, _, t=t, y=y):
            g2 = virt[x] ^ hp
            mine = jnp.where(row_blocks[t] == x, y, 0.0)
            for half in range(nat // 256):

                @pl.when(counts[g2] > 4 * half)
                def _():
                    load_rows(s2, g2, half)
                    zs[t, :TILE] += dot3(dot_nn, mine[:, 256 * half : 256 * half + 256])

            return 0

        lax.fori_loop(firsts[t], last + 1, second_product, 0)

    for t in range(2):
        for k in range(8):
            if slots != SLOTS:
                z_ref[t, k] = zs[t, :TILE, pl.ds(128 * k, 128)]
                continue
            j = k // 2
            top = zs[t, 0:HALF, pl.ds(128 * j, 128)]
            bottom = zs[t, HALF : 2 * HALF, pl.ds(128 * j, 128)]
            if k % 2 == 0:
                z_ref[t, k] = jnp.where(left, top, pltpu.roll(bottom, SLOTS, 1))
            else:
                z_ref[t, k] = jnp.where(left, pltpu.roll(top, SLOTS, 1), bottom)


def scatter_kernel(slots, virt, pair, z_ref, out_ref, parts, low_ref, high_ref, send, recv, near):
    r, s, o = coords()
    y, rest = r // 8, r % 8
    alone = jnp.where(y == o, 1, 0)
    barrier = pltpu.get_barrier_semaphore()

    def greet(e, k):
        pl.semaphore_signal(
            barrier, inc=1, device_id=(o * 8 + rest, (s + k) % 8, e), device_id_type=MESH
        )

    def describe(e, k):
        return pltpu.make_async_remote_copy(
            src_ref=z_ref.at[e, (s + k) % 8],
            dst_ref=parts.at[o, s],
            send_sem=send.at[8 * e + k],
            recv_sem=recv.at[8 * o + k],
            device_id=(e * 8 + rest, (s + k) % 8, y),
            device_id_type=MESH,
        )

    def sender(e, k):
        describe(e, k).start()

    def receive(e, k):
        spot = parts.at[e, (s - k + 8) % 8]
        pltpu.make_async_remote_copy(
            src_ref=spot,
            dst_ref=spot,
            send_sem=send.at[0],
            recv_sem=recv.at[8 * e + k],
            device_id=(o * 8 + rest, (s + 1) % 8, e),
            device_id_type=MESH,
        ).wait_recv()

    def finish(e, k):
        describe(e, k).wait_send()

    def each(fn, mine):
        for k in (4, 3, 5, 2, 6, 1, 7, 0):
            for e in range(2):
                if k:
                    fn(e, k)
                else:
                    pl.when(jnp.logical_or(y != o, mine != e))(functools.partial(fn, e, k))

    each(greet, o)
    pl.semaphore_wait(barrier, 16 - alone)
    each(sender, y)

    @pl.when(y == o)
    def _():
        copy = pltpu.make_async_copy(z_ref.at[y, s], parts.at[o, s], near.at[0])
        copy.start()
        copy.wait()

    first = (STRIPS * r) >> 3
    d, block, label, rank = column_facts(virt, s, (1, WIDE))
    each(receive, o)
    total = parts[0, 0]
    for k in range(1, 16):
        total = total + parts[k // 8, k % 8]
    hi, lo = split(0.5 * total)
    rows = packed_rows(slots)
    row = iota((rows, 1), 0)
    for half in range(128 // slots):
        spread = jnp.where(iota((128, WIDE), 0) == rank + slots * half, 1.0, 0.0).astype(BF16)
        dense = dot_nn(hi, spread) + dot_nn(lo, spread)
        row_block = (TILE * r + rows * half + row) >> 6
        keep = label == (row_label(virt, row_block, first) ^ pair[o])
        dense = jnp.where(keep, dense, 0.0)
        low_ref[rows * half : rows * half + rows, :] = dense[:, :128]
        high_ref[rows * half : rows * half + rows, :] = jnp.concatenate(
            [dense[:, 128:], jnp.zeros((rows, 256 - WIDE), F32)], axis=1
        )
    lines = []
    for v in range(8):
        low, high = low_ref[pl.ds(v, STRIPS, stride=8), :], high_ref[pl.ds(v, STRIPS, stride=8), :]
        lines.append(jnp.concatenate([low, high[:, : WIDE - 128]], axis=1))
    for k in range(STRIPS):
        v, w = (128 * k) // WIDE, (128 * k) % WIDE
        piece = lines[v][:, w : min(WIDE, w + 128)]
        if w + 128 > WIDE:
            piece = jnp.concatenate([piece, lines[v + 1][:, : w + 128 - WIDE]], axis=1)
        out_ref[pl.ds(k, STRIPS, stride=STRIPS), :] = piece
    each(finish, y)


def smem(n):
    return [pl.BlockSpec(memory_space=pltpu.SMEM)] * n


def vmem(n):
    return [pl.BlockSpec(memory_space=pltpu.VMEM)] * n


def shape(*dims):
    return jax.ShapeDtypeStruct(dims, F32)


def run_gather(slots, virt, pair, aux, pat, a, b):
    rows, nat = packed_rows(slots), 8 * slots
    full = pltpu.VMEM((2, 4, 2, 8, rows, 128), F32)
    return pl.pallas_call(
        functools.partial(gather_kernel, slots),
        out_shape=(
            shape(VIRTUALS + BLOCK_WIDTH, nat),
            shape(VIRTUALS + BLOCK_WIDTH, nat),
            shape(WIDE, nat),
            jax.ShapeDtypeStruct((8, WIDE), I32),
            jax.ShapeDtypeStruct((8, 128, WIDE), BF16),
            jax.ShapeDtypeStruct((8, nat, WIDE), BF16),
        ),
        in_specs=smem(4) + [pl.BlockSpec(memory_space=pl.ANY)] + vmem(1),
        out_specs=tuple(vmem(6)),
        scratch_shapes=[
            full,
            full,
            pltpu.VMEM((2 * 121, 1, 128), F32),
            pltpu.VMEM((8 * TILE + 8, 128), F32),
            pltpu.VMEM((10, rows, 128), F32),
            pltpu.SemaphoreType.DMA((64,)),
            pltpu.SemaphoreType.DMA((64,)),
            pltpu.SemaphoreType.DMA((3,)),
        ],
        compiler_params=pltpu.CompilerParams(
            collective_id=0 if slots == SLOTS else 2,
            has_side_effects=True,
            vmem_limit_bytes=(20 if slots == SLOTS else 36) * MIB,
        ),
    )(virt, pair, aux, pat, a, b)


def run_product(slots, virt, pair, aux, *gathered):
    nat = 8 * slots
    return pl.pallas_call(
        functools.partial(product_kernel, slots),
        out_shape=shape(2, 8, packed_rows(slots), 128),
        in_specs=smem(3) + vmem(6),
        out_specs=vmem(1)[0],
        scratch_shapes=[
            pltpu.VMEM((2, TILE, nat), F32),
            pltpu.VMEM((2, TILE, nat), F32),
            pltpu.VMEM((2, 2 * HALF, nat), F32),
            pltpu.VMEM((256, nat), BF16),
            pltpu.VMEM((256, nat), BF16),
            pltpu.SMEM((slots,), I32),
            pltpu.SMEM((8,), I32),
        ],
        compiler_params=pltpu.CompilerParams(vmem_limit_bytes=(20 if slots == SLOTS else 36) * MIB),
    )(virt, pair, aux, *gathered)


def run_scatter(slots, virt, pair, z):
    return pl.pallas_call(
        functools.partial(scatter_kernel, slots),
        out_shape=shape(121, 128),
        in_specs=smem(2) + vmem(1),
        out_specs=vmem(1)[0],
        scratch_shapes=[
            pltpu.VMEM((2, 8, packed_rows(slots), 128), F32),
            pltpu.VMEM((2 * HALF, 128), F32),
            pltpu.VMEM((2 * HALF, 128), F32),
            pltpu.SemaphoreType.DMA((16,)),
            pltpu.SemaphoreType.DMA((16,)),
            pltpu.SemaphoreType.DMA((1,)),
        ],
        compiler_params=pltpu.CompilerParams(
            collective_id=1 if slots == SLOTS else 3, has_side_effects=True, vmem_limit_bytes=16 * MIB
        ),
    )(virt, pair, z)


def packed_path(slots, amplitudes, aux_factor, virt, pair, aux, pat):
    gathered = run_gather(
        slots, virt, pair, aux, pat, amplitudes.reshape(242, 1, 128), aux_factor.reshape(968, 128)
    )
    z = run_product(slots, virt, pair, aux, *gathered)
    return run_scatter(slots, virt, pair, z).reshape(1, 1, 1, TILE * WIDE)


def choose_kernel(virt, out_ref):
    group = iota((8, 1), 0)
    lane = iota((8, 128), 1)
    totals = jnp.zeros((8, 128), I32)
    for b in range(BLOCKS):
        share = cols_before(BLOCK_WIDTH * (b + 1), group) - cols_before(BLOCK_WIDTH * b, group)
        totals = totals + jnp.where(lane == virt[b], share, 0)
    widest = jnp.max(totals)
    out_ref[0] = jnp.where(widest > SLOTS, 1, 0) + jnp.where(widest > 128, 1, 0)


def choose(virt):
    return pl.pallas_call(
        choose_kernel,
        out_shape=jax.ShapeDtypeStruct((1,), I32),
        in_specs=smem(1),
        out_specs=smem(1)[0],
    )(virt)[0]


def block_onehot(indices, block_count):
    return indices[..., None] // BLOCK_WIDTH == jnp.arange(block_count, dtype=jnp.int32)


def label_lookup(hot_table, virt_irrep):
    return jnp.sum(jnp.where(hot_table, virt_irrep, 0), axis=-1)


def dense_path(amplitudes, aux_factor, virt_irrep, pair_irrep, aux_irrep, block_pattern):
    tile_count = lax.axis_size("row")
    col_count = lax.axis_size("col")
    local_rows = VIRTUALS // tile_count
    sub_width = local_rows // col_count
    amplitudes = amplitudes.reshape(amplitudes.shape[0], local_rows, tile_count, sub_width)
    aux_factor = aux_factor.reshape(aux_factor.shape[0], local_rows, tile_count, sub_width)
    block_count = virt_irrep.shape[0]
    row_index = lax.axis_index("row") * local_rows + jnp.arange(local_rows, dtype=jnp.int32)
    col_index = (
        jnp.arange(tile_count, dtype=jnp.int32)[:, None] * local_rows
        + lax.axis_index("col") * sub_width
        + jnp.arange(sub_width, dtype=jnp.int32)[None, :]
    )
    row_hot = block_onehot(row_index, block_count)
    col_hot = block_onehot(col_index, block_count)
    product = jnp.bitwise_xor(
        label_lookup(row_hot, virt_irrep)[:, None, None], label_lookup(col_hot, virt_irrep)[None]
    )
    kept_mask = product[None] == pair_irrep[:, None, None, None]
    masked = jnp.where(kept_mask, amplitudes, 0.0)
    pattern = (block_pattern * block_pattern.T).astype(jnp.float32)
    screen = (
        jnp.einsum(
            "ak,kl,itl->ait", row_hot.astype(jnp.float32), pattern, col_hot.astype(jnp.float32)
        )
        > 0.5
    )
    aux_here = aux_factor.shape[0]
    aux_labels = lax.dynamic_slice_in_dim(aux_irrep, lax.axis_index("occ") * aux_here, aux_here, 0)
    aux_mask = jnp.logical_and(screen[None], product[None] == aux_labels[:, None, None, None])
    factor = jnp.where(aux_mask, aux_factor, 0.0)
    half_pairs = masked.shape[0] // lax.axis_size("occ")
    masked = lax.dynamic_slice_in_dim(masked, lax.axis_index("occ") * half_pairs, half_pairs, 0)
    factor = lax.all_gather(factor, "occ", axis=0, tiled=True)
    pair_count = masked.shape[0]
    aux_count = factor.shape[0]
    split_view = masked.reshape(pair_count, col_count, sub_width, tile_count, sub_width)
    swapped = lax.all_to_all(
        lax.all_to_all(split_view, "row", split_axis=3, concat_axis=3, tiled=True),
        "col",
        split_axis=1,
        concat_axis=4,
        tiled=True,
    )
    mirrored = swapped.reshape(pair_count, sub_width, tile_count, local_rows).transpose(0, 3, 2, 1)
    antisym = masked - mirrored
    columns = lax.all_gather(factor, "row", axis=1, tiled=True)
    columns = columns.reshape(aux_count, tile_count, local_rows, tile_count * sub_width)
    rows_panel = lax.all_gather(factor, "col", axis=3, tiled=True).reshape(
        aux_count, local_rows, tile_count * local_rows
    )
    chosen = columns
    contracted = jnp.einsum(
        "pcik,qikn->qpcn",
        lax.all_gather(antisym, "col", axis=3, tiled=True),
        chosen,
        precision=lax.Precision.HIGHEST,
    )
    chosen = rows_panel
    summed = lax.psum_scatter(
        jnp.einsum("qca,qpcn->apn", chosen, contracted, precision=lax.Precision.HIGHEST),
        "row",
        scatter_dimension=0,
        tiled=True,
    )
    pairs_out = summed.shape[1]
    result = (
        (0.5 * summed).reshape(local_rows, pairs_out, tile_count, sub_width).transpose(1, 0, 2, 3)
    )
    return result.reshape(pairs_out, 1, 1, local_rows * tile_count * sub_width)


def per_device(*args):
    paths = [functools.partial(packed_path, SLOTS), functools.partial(packed_path, 128), dense_path]
    return lax.switch(choose(args[2]), paths, *args)


def solution(mesh):
    placed = (P(None, "row", "col", None), P("occ", "row", "col", None), P(), P(), P(), P())
    return jax.shard_map(
        per_device,
        mesh=mesh,
        in_specs=placed,
        out_specs=P("occ", "row", "col", None),
        check_vma=False,
    )
```

```python
import functools

import jax
import jax.numpy as jnp
from jax import lax
from jax.experimental import pallas as pl
from jax.experimental.pallas import tpu as pltpu
from jax.sharding import PartitionSpec as P

VIRTUALS = 1408
BLOCK_WIDTH = 64
BLOCKS = 22
LABELS = 8
ROWS, COLS = 16, 8
TILE = 88
WIDE = 176
STRIPS = 11
SLOTS = 64
HALF = 48
MESH = pl.DeviceIdType.MESH
MIB = 1 << 20
F32, BF16, I32 = jnp.float32, jnp.bfloat16, jnp.int32


def coords():
    return lax.axis_index("row"), lax.axis_index("col"), lax.axis_index("occ")


def iota(shape, dim):
    return lax.broadcasted_iota(I32, shape, dim)


def div11(v):
    return (v * 5958) >> 16


def split(x):
    hi = x.astype(BF16)
    return hi, (x - hi.astype(F32)).astype(BF16)


def packed_rows(slots):
    return HALF if slots == SLOTS else TILE


def dot_nn(a, b):
    return lax.dot_general(a, b, (((1,), (0,)), ((), ())), preferred_element_type=F32)


def dot_nt(a, b):
    return lax.dot_general(a, b, (((1,), (1,)), ((), ())), preferred_element_type=F32)


def cols_before(n, s):
    return (n // TILE) * STRIPS + jnp.clip(n % TILE - STRIPS * s, 0, STRIPS)


def column_facts(virt, s, shape):
    w = iota(shape, 1)
    d = w + 77 * div11(w) + STRIPS * s
    block = d >> 6
    before = [cols_before(BLOCK_WIDTH * b, s) for b in range(BLOCKS + 1)]
    labels = [virt[b] for b in range(BLOCKS)]
    label = jnp.zeros(shape, I32)
    rank = w
    for b in range(BLOCKS):
        base = -before[b]
        for e in range(b):
            base = base + jnp.where(labels[e] == labels[b], before[e + 1] - before[e], 0)
        here = block == b
        label = jnp.where(here, labels[b], label)
        rank = jnp.where(here, w + base, rank)
    return d, block, label, rank


def row_label(virt, block, first):
    label = virt[first]
    for k in (1, 2):
        label = jnp.where(block == first + k, virt[jnp.minimum(first + k, BLOCKS - 1)], label)
    return label


def pack_tiles(slots, virt, pair, aux, pat, a_ref, b_ref, d_ref, packed, send_a, send_b):
    r, s, o = coords()
    first = (STRIPS * r) >> 3
    d, block, label, rank = column_facts(virt, s, (1, WIDE))
    sel = jnp.where((iota((128, WIDE), 0) & (slots - 1)) == rank, 1.0, 0.0).astype(BF16)
    left = iota((HALF, 128), 1) < SLOTS

    def pack(src, count, keep, base):
        n = count * STRIPS
        if len(src.shape) == 3:
            lines = [src[pl.ds(k, n, stride=STRIPS), 0, :] for k in range(STRIPS)]
        else:
            lines = [src[pl.ds(k, n, stride=STRIPS), :] for k in range(STRIPS)]
        for v in range(8):
            start = WIDE * v
            low, off = start // 128, start % 128
            last = (start + WIDE - 1) // 128
            tile = jnp.concatenate(lines[low : last + 1], axis=1)[:, off : off + WIDE]
            hi, lo = split(jnp.where(keep, tile, 0.0))
            d_ref[pl.ds(v, n, stride=8), :] = dot_nt(hi, sel) + dot_nt(lo, sel)
        d_ref[n * 8 : n * 8 + 8, :] = jnp.zeros((8, 128), F32)
        for k in range(count):
            if slots == SLOTS:
                top = d_ref[pl.ds(TILE * k, HALF), :]
                bottom = d_ref[pl.ds(TILE * k + HALF, HALF), :]
                packed[base + k] = jnp.where(left, top, bottom)
            else:
                packed[base + k] = d_ref[pl.ds(TILE * k, TILE), :]

    row = iota((2 * STRIPS, 1), 0)
    p = jnp.where(row >= STRIPS, 1, 0)
    row_block = (STRIPS * r + row - STRIPS * p) >> 3
    keep = label == (row_label(virt, row_block, first) ^ jnp.where(p == 1, pair[1], pair[0]))
    pack(a_ref, 2, keep, 8)
    send_a()

    screens = []
    for k in range(3):
        x = jnp.minimum(first + k, BLOCKS - 1)
        flag = jnp.zeros((1, WIDE), I32)
        for b in range(BLOCKS):
            flag = jnp.where(block == b, pat[x, b] * pat[b, x], flag)
        screens.append(flag)
    row = iota((TILE, 1), 0)
    q = div11(row)
    row_block = (STRIPS * r + row - STRIPS * q) >> 3
    aux_row = jnp.zeros((TILE, 1), I32)
    for k in range(8):
        aux_row = jnp.where(q == k, aux[8 * o + k], aux_row)
    screen = jnp.where(
        row_block == first, screens[0], jnp.where(row_block == first + 1, screens[1], screens[2])
    )
    target = row_label(virt, row_block, first) ^ aux_row
    pack(b_ref, 8, jnp.logical_and(label == target, screen > 0), 0)
    send_b()


def to_natural(slots, x, target, label, spread, pick):
    hi, lo = split(x)
    both = jnp.concatenate([hi, lo], axis=0)
    target = jnp.concatenate([target, target], axis=0)
    total = jnp.zeros((both.shape[0], 8 * slots), F32)
    for k in range(8):
        j = (slots * k) // 128
        dense = dot_nn(both[:, 128 * j : 128 * j + 128], spread[k])
        dense = jnp.where(label[k : k + 1] == target, dense, 0.0).astype(BF16)
        total = total + dot_nt(dense, pick[k])
    return total[: x.shape[0]] + total[x.shape[0] :]


def my_tiles(r):
    tiles = (r % 8, 8 + r % 8)
    bases = [pl.multiple_of(t * TILE, 8) for t in tiles]
    firsts = [(STRIPS * t) >> 3 for t in tiles]
    row_blocks = [(t * TILE + iota((TILE, 1), 0)) >> 6 for t in tiles]
    return tiles, bases, firsts, row_blocks


def tile_labels(virt, firsts, row_blocks):
    return jnp.concatenate([row_label(virt, b, f) for b, f in zip(row_blocks, firsts)], axis=0)


def gather_kernel(
    slots,
    virt,
    pair,
    aux,
    pat,
    a_ref,
    b_ref,
    a2,
    s2,
    own_natural,
    label_ref,
    spread_ref,
    pick_ref,
    aa_ref,
    sa_ref,
    a_lines,
    d_ref,
    packed,
    send,
    recv,
    near,
):
    r, s, o = coords()
    c, x, y = r % 2, (r // 2) % 4, r // 8

    def at(cc, xx, yy, ss):
        return (yy * 8 + xx * 2 + cc, ss, o)

    zs = {k: at(c, x, y, (s + k) % 8) for k in range(1, 8)}
    planes = {
        (e, k): at(c, (x + k) % 4, (y + e) % 2, s) for e in range(2) for k in range(4) if e + k
    }
    sibling = at(1 - c, x, y, s)
    barrier = pltpu.get_barrier_semaphore()
    for peer in [*zs.values(), *planes.values(), sibling]:
        pl.semaphore_signal(barrier, inc=1, device_id=peer, device_id_type=MESH)

    kinds = {}
    copies = []

    def number(kind):
        return kinds.setdefault(kind, len(kinds))

    def describe(src, dst, peer, kind):
        n = number(kind)
        return pltpu.make_async_remote_copy(
            src_ref=src,
            dst_ref=dst,
            send_sem=send.at[n],
            recv_sem=recv.at[n],
            device_id=peer,
            device_id_type=MESH,
        )

    def put(src, dst, peer, *kind):
        copies.append(describe(src, dst, peer, kind))
        copies[-1].start()

    def arrived(ref, *kind):
        describe(ref, ref, sibling, kind).wait_recv()

    def share(ref, *kind):
        put(ref, ref, sibling, "core", *kind)

    def sign(way, k):
        return k if way else -k

    def a_block(k, ch, cc=c):
        return aa_ref.at[cc, 2 * ch : 2 * ch + 2, :, (s + k + 8) % 8]

    def s_block(k, e, cc=c):
        return sa_ref.at[cc, (x + k + 4) % 4, (y + e) % 2]

    def send_a():
        pl.semaphore_wait(barrier, 15)
        for (e, k), peer in planes.items():
            put(packed.at[8 + (y + e) % 2], aa_ref.at[c, x, y, s], peer, "ax", e, k)
        own = pltpu.make_async_copy(packed.at[8 + y], aa_ref.at[c, x, y, s], near.at[0])
        own.start()
        own.wait()

    def send_b():
        for k in (4, 3, 5, 2, 6, 1, 7):
            put(packed.at[(s + k) % 8], sa_ref.at[c, x, y, s], zs[k], "sz", k)
        own = pltpu.make_async_copy(packed.at[s], sa_ref.at[c, x, y, s], near.at[1])
        own.start()
        own.wait()

    amplitudes = pltpu.make_async_copy(a_ref, a_lines, near.at[2])
    amplitudes.start()
    amplitudes.wait()
    pack_tiles(slots, virt, pair, aux, pat, a_lines, b_ref, d_ref, packed, send_a, send_b)

    def tile_base(xx, yy, cc):
        return pl.multiple_of((yy * 8 + xx * 2 + cc) * TILE, 8)

    half_lanes = iota((HALF, 128), 1) < SLOTS

    def take_a(k, ch, cc=c):
        ss = (s + k + 8) % 8
        lane = pl.multiple_of(128 * (ss // (128 // slots)), 128)

        def take(n, _):
            xx, yy = 2 * ch + n // 2, n % 2
            base = tile_base(xx, yy, cc)
            piece = aa_ref[cc, xx, yy, ss]
            if slots != SLOTS:
                a2[pl.ds(base, TILE), pl.ds(lane, 128)] = piece
                return 0
            odd = ss % 2 == 1
            turned = pltpu.roll(piece, SLOTS, 1)
            top = jnp.where(odd, turned, piece)
            bottom = jnp.where(odd, piece, turned)
            mine = jnp.logical_xor(half_lanes, odd)
            for at_row, value, n_rows in ((base, top, HALF), (base + HALF, bottom, TILE - HALF)):
                rows = pl.ds(pl.multiple_of(at_row, 8), n_rows)
                there = a2[rows, pl.ds(lane, 128)]
                a2[rows, pl.ds(lane, 128)] = jnp.where(mine[:n_rows], value[:n_rows], there)
            return 0

        lax.fori_loop(0, 4, take, 0)

    def take_s(k, e, cc=c):
        xx, yy = (x + k + 4) % 4, (y + e) % 2
        base = tile_base(xx, yy, cc)
        if slots != SLOTS:
            for j in range(8):
                s2[pl.ds(base, TILE), pl.ds(128 * j, 128)] = sa_ref[cc, xx, yy, j]
            return
        for j in range(4):
            even, odd = sa_ref[cc, xx, yy, 2 * j], sa_ref[cc, xx, yy, 2 * j + 1]
            top = jnp.where(half_lanes, even, pltpu.roll(odd, SLOTS, 1))
            bottom = jnp.where(half_lanes, pltpu.roll(even, SLOTS, 1), odd)
            s2[pl.ds(base, HALF), pl.ds(128 * j, 128)] = top
            s2[pl.ds(base + HALF, TILE - HALF), pl.ds(128 * j, 128)] = bottom[: TILE - HALF]

    def a_ring(h):
        for ch in range(2):
            for way in range(2):
                block = a_block(sign(1 - way, h), ch)
                if h and (h < 4 or ch != way):
                    arrived(block, "az", way, h - 1, ch)
                if h < 3 or (h == 3 and ch != way):
                    put(block, block, zs[1 if way else 7], "az", way, h, ch)
                if h and (h < 4 or ch != way):
                    share(block, "az", way, h - 1, ch)
                if h == 0 and way == 0:
                    share(block, "own", ch)

    def a_take(h):
        for ch in range(2):
            for way in range(2):
                if (h and (h < 4 or ch != way)) or (h == 0 and way == 0):
                    take_a(sign(1 - way, h), ch)

    def a_sibling(h):
        for ch in range(2):
            if h == 0:
                arrived(a_block(0, ch, 1 - c), "core", "own", ch)
                take_a(0, ch, 1 - c)
                continue
            for way in range(2):
                if h < 4 or ch != way:
                    k = sign(1 - way, h)
                    arrived(a_block(k, ch, 1 - c), "core", "az", way, h - 1, ch)
                    take_a(k, ch, 1 - c)

    def s_arrival(e):
        for way in range(2):
            block = s_block(sign(1 - way, 1), e)
            arrived(block, "sx", way, e)
            if e != way:
                put(block, block, planes[0, 1 if way else 3], "sxx", way)
            share(block, "sx", way, e)

    def s_take(e):
        for way in range(2):
            take_s(sign(1 - way, 1), e)

    def s_sibling(e):
        for way in range(2):
            k = sign(1 - way, 1)
            arrived(s_block(k, e, 1 - c), "core", "sx", way, e)
            take_s(k, e, 1 - c)

    def s_start(e):
        block = s_block(0, e)
        for way in range(2):
            put(block, block, planes[0, 1 if way else 3], "sx", way, e)
        share(block, "sy", e)

    def s_start_sibling(e):
        arrived(s_block(0, e, 1 - c), "core", "sy", e)
        take_s(0, e, 1 - c)

    for e, k in planes:
        arrived(aa_ref.at[c, (x - k + 4) % 4, (y + e) % 2, s], "ax", e, k)
    a_ring(0)

    group = iota((8, 1), 0)
    d, block, label, rank = column_facts(virt, group, (8, WIDE))
    place = jnp.zeros((8, WIDE), I32)
    for b in range(BLOCKS):
        seen = 0
        for e in range(b):
            seen = seen + jnp.where(virt[e] == virt[b], 1, 0)
        place = jnp.where(block == b, seen, place)
    natural = place * BLOCK_WIDTH + (d & (BLOCK_WIDTH - 1))
    label_ref[...] = label
    for k in range(8):
        shift = (slots * k) % 128
        spread = jnp.where(iota((128, WIDE), 0) == rank[k : k + 1] + shift, 1.0, 0.0)
        spread_ref[k] = spread.astype(BF16)
    a2[...] = jnp.zeros_like(a2)
    s2[VIRTUALS:, :] = jnp.zeros((BLOCK_WIDTH, 8 * slots), F32)

    def build_picks(ks):
        for k in ks:
            pick = jnp.where(iota((8 * slots, WIDE), 0) == natural[k : k + 1], 1.0, 0.0)
            pick_ref[k] = pick.astype(BF16)

    build_picks(range(4))
    for k in (1, 7, 2, 6, 3, 5, 4):
        arrived(sa_ref.at[c, x, y, (s - k + 8) % 8], "sz", k)
    put(s_block(0, 0), s_block(0, 0), planes[1, 0], "sy")
    s_start(0)
    a_take(0)
    take_s(0, 0)
    build_picks(range(4, 8))
    a_ring(1)
    arrived(s_block(0, 1), "sy")
    s_start(1)
    take_s(0, 1)
    tiles, bases, firsts, row_blocks = my_tiles(r)
    target = tile_labels(virt, firsts, row_blocks) ^ aux[8 * o + s]
    own = jnp.concatenate([s2[pl.ds(b, TILE), :] for b in bases], axis=0)
    own_natural[...] = to_natural(slots, own, target, label, spread_ref, pick_ref)
    s_arrival(0)
    a_take(1)
    s_start_sibling(0)
    s_start_sibling(1)
    a_ring(2)
    s_take(0)
    a_sibling(0)
    a_sibling(1)
    a_take(2)
    s_arrival(1)
    a_ring(3)
    s_take(1)
    a_take(3)
    s_sibling(0)
    a_sibling(2)
    for way in range(2):
        block = s_block(2, 1 - way)
        arrived(block, "sxx", way)
        share(block, "sxx", way)
    a_ring(4)
    s_sibling(1)
    a_sibling(3)
    for way in range(2):
        take_s(2, 1 - way)
    a_take(4)
    for way in range(2):
        arrived(s_block(2, 1 - way, 1 - c), "core", "sxx", way)
        take_s(2, 1 - way, 1 - c)
    a_sibling(4)
    for copy in copies:
        copy.wait_send()


def product_kernel(
    slots,
    virt,
    pair,
    aux,
    a2,
    s2,
    own_natural,
    label_ref,
    spread_ref,
    pick_ref,
    z_ref,
    v1,
    v2,
    zs,
    whi,
    wlo,
    lists,
    counts,
):
    r, s, o = coords()
    nat, per_label = 8 * slots, slots // 8
    h = aux[8 * o + s]
    hp = h ^ pair[r // 8]
    left = iota((HALF, 128), 1) < SLOTS
    for g in range(LABELS):
        counts[g] = 0
        for j in range(per_label):
            lists[per_label * g + j] = BLOCKS
    for b in range(BLOCKS):
        g = virt[b]
        n = counts[g]
        lists[per_label * g + jnp.minimum(n, per_label - 1)] = b
        counts[g] = n + 1
    tiles, bases, firsts, row_blocks = my_tiles(r)
    labels = tile_labels(virt, firsts, row_blocks)

    def load_rows(src, g, half):
        for j in range(4):
            b = lists[per_label * g + 4 * half + j]
            hi, lo = split(src[pl.ds(pl.multiple_of(b * BLOCK_WIDTH, BLOCK_WIDTH), BLOCK_WIDTH), :])
            whi[pl.ds(BLOCK_WIDTH * j, BLOCK_WIDTH), :] = hi
            wlo[pl.ds(BLOCK_WIDTH * j, BLOCK_WIDTH), :] = lo

    def dot3(dot, a):
        tall = 2 * HALF
        hi, lo = split(jnp.concatenate([a, jnp.zeros((tall - TILE, a.shape[1]), F32)], axis=0))
        both = dot(jnp.concatenate([hi, lo], axis=0), whi[...])
        return (both[:tall] + both[tall:] + dot(hi, wlo[...]))[:TILE]

    v1[...] = jnp.zeros_like(v1)
    v2[...] = jnp.zeros_like(v2)
    zs[...] = jnp.zeros_like(zs)
    for t in range(2):
        last = (STRIPS * tiles[t] + STRIPS - 1) >> 3

        def first_product(x, _, t=t):
            g1 = virt[x] ^ h
            g2 = virt[x] ^ hp
            here = row_blocks[t] == x
            mine = jnp.where(here, s2[pl.ds(bases[t], TILE), :], 0.0)
            mine_natural = jnp.where(here, own_natural[TILE * t : TILE * t + TILE, :], 0.0)
            for half in range(nat // 256):
                part = slice(256 * half, 256 * half + 256)

                @pl.when(counts[g1] > 4 * half)
                def _():
                    load_rows(a2, g1, half)
                    v2[t] += dot3(dot_nn, mine_natural[:, part])

                @pl.when(counts[g2] > 4 * half)
                def _():
                    load_rows(a2, g2, half)
                    v1[t, :, part] += dot3(dot_nt, mine)

            return 0

        lax.fori_loop(firsts[t], last + 1, first_product, 0)

    v2_rows = jnp.concatenate([v2[0], v2[1]], axis=0)
    turned = to_natural(slots, v2_rows, labels ^ hp, label_ref[...], spread_ref, pick_ref)
    for t in range(2):
        last = (STRIPS * tiles[t] + STRIPS - 1) >> 3
        y = turned[TILE * t : TILE * t + TILE] - v1[t]

        def second_product(x, _, t=t, y=y):
            g2 = virt[x] ^ hp
            mine = jnp.where(row_blocks[t] == x, y, 0.0)
            for half in range(nat // 256):

                @pl.when(counts[g2] > 4 * half)
                def _():
                    load_rows(s2, g2, half)
                    zs[t, :TILE] += dot3(dot_nn, mine[:, 256 * half : 256 * half + 256])

            return 0

        lax.fori_loop(firsts[t], last + 1, second_product, 0)

    for t in range(2):
        for k in range(8):
            if slots != SLOTS:
                z_ref[t, k] = zs[t, :TILE, pl.ds(128 * k, 128)]
                continue
            j = k // 2
            top = zs[t, 0:HALF, pl.ds(128 * j, 128)]
            bottom = zs[t, HALF : 2 * HALF, pl.ds(128 * j, 128)]
            if k % 2 == 0:
                z_ref[t, k] = jnp.where(left, top, pltpu.roll(bottom, SLOTS, 1))
            else:
                z_ref[t, k] = jnp.where(left, pltpu.roll(top, SLOTS, 1), bottom)


def scatter_kernel(slots, virt, pair, z_ref, out_ref, parts, low_ref, high_ref, send, recv, near):
    r, s, o = coords()
    y, rest = r // 8, r % 8
    alone = jnp.where(y == o, 1, 0)
    barrier = pltpu.get_barrier_semaphore()

    def greet(e, k):
        pl.semaphore_signal(
            barrier, inc=1, device_id=(o * 8 + rest, (s + k) % 8, e), device_id_type=MESH
        )

    def describe(e, k):
        return pltpu.make_async_remote_copy(
            src_ref=z_ref.at[e, (s + k) % 8],
            dst_ref=parts.at[o, s],
            send_sem=send.at[8 * e + k],
            recv_sem=recv.at[8 * o + k],
            device_id=(e * 8 + rest, (s + k) % 8, y),
            device_id_type=MESH,
        )

    def sender(e, k):
        describe(e, k).start()

    def receive(e, k):
        spot = parts.at[e, (s - k + 8) % 8]
        pltpu.make_async_remote_copy(
            src_ref=spot,
            dst_ref=spot,
            send_sem=send.at[0],
            recv_sem=recv.at[8 * e + k],
            device_id=(o * 8 + rest, (s + 1) % 8, e),
            device_id_type=MESH,
        ).wait_recv()

    def finish(e, k):
        describe(e, k).wait_send()

    def each(fn, mine):
        for k in (4, 3, 5, 2, 6, 1, 7, 0):
            for e in range(2):
                if k:
                    fn(e, k)
                else:
                    pl.when(jnp.logical_or(y != o, mine != e))(functools.partial(fn, e, k))

    each(greet, o)
    pl.semaphore_wait(barrier, 16 - alone)
    each(sender, y)

    @pl.when(y == o)
    def _():
        copy = pltpu.make_async_copy(z_ref.at[y, s], parts.at[o, s], near.at[0])
        copy.start()
        copy.wait()

    first = (STRIPS * r) >> 3
    d, block, label, rank = column_facts(virt, s, (1, WIDE))
    each(receive, o)
    total = parts[0, 0]
    for k in range(1, 16):
        total = total + parts[k // 8, k % 8]
    hi, lo = split(0.5 * total)
    rows = packed_rows(slots)
    row = iota((rows, 1), 0)
    for half in range(128 // slots):
        spread = jnp.where(iota((128, WIDE), 0) == rank + slots * half, 1.0, 0.0).astype(BF16)
        dense = dot_nn(hi, spread) + dot_nn(lo, spread)
        row_block = (TILE * r + rows * half + row) >> 6
        keep = label == (row_label(virt, row_block, first) ^ pair[o])
        dense = jnp.where(keep, dense, 0.0)
        low_ref[rows * half : rows * half + rows, :] = dense[:, :128]
        high_ref[rows * half : rows * half + rows, :] = jnp.concatenate(
            [dense[:, 128:], jnp.zeros((rows, 256 - WIDE), F32)], axis=1
        )
    lines = []
    for v in range(8):
        low, high = low_ref[pl.ds(v, STRIPS, stride=8), :], high_ref[pl.ds(v, STRIPS, stride=8), :]
        lines.append(jnp.concatenate([low, high[:, : WIDE - 128]], axis=1))
    for k in range(STRIPS):
        v, w = (128 * k) // WIDE, (128 * k) % WIDE
        piece = lines[v][:, w : min(WIDE, w + 128)]
        if w + 128 > WIDE:
            piece = jnp.concatenate([piece, lines[v + 1][:, : w + 128 - WIDE]], axis=1)
        out_ref[pl.ds(k, STRIPS, stride=STRIPS), :] = piece
    each(finish, y)


def smem(n):
    return [pl.BlockSpec(memory_space=pltpu.SMEM)] * n


def vmem(n):
    return [pl.BlockSpec(memory_space=pltpu.VMEM)] * n


def shape(*dims):
    return jax.ShapeDtypeStruct(dims, F32)


def run_gather(slots, virt, pair, aux, pat, a, b):
    rows, nat = packed_rows(slots), 8 * slots
    full = pltpu.VMEM((2, 4, 2, 8, rows, 128), F32)
    return pl.pallas_call(
        functools.partial(gather_kernel, slots),
        out_shape=(
            shape(VIRTUALS + BLOCK_WIDTH, nat),
            shape(VIRTUALS + BLOCK_WIDTH, nat),
            shape(WIDE, nat),
            jax.ShapeDtypeStruct((8, WIDE), I32),
            jax.ShapeDtypeStruct((8, 128, WIDE), BF16),
            jax.ShapeDtypeStruct((8, nat, WIDE), BF16),
        ),
        in_specs=smem(4) + [pl.BlockSpec(memory_space=pl.ANY)] + vmem(1),
        out_specs=tuple(vmem(6)),
        scratch_shapes=[
            full,
            full,
            pltpu.VMEM((2 * 121, 1, 128), F32),
            pltpu.VMEM((8 * TILE + 8, 128), F32),
            pltpu.VMEM((10, rows, 128), F32),
            pltpu.SemaphoreType.DMA((64,)),
            pltpu.SemaphoreType.DMA((64,)),
            pltpu.SemaphoreType.DMA((3,)),
        ],
        compiler_params=pltpu.CompilerParams(
            collective_id=0 if slots == SLOTS else 2,
            has_side_effects=True,
            vmem_limit_bytes=(20 if slots == SLOTS else 36) * MIB,
        ),
    )(virt, pair, aux, pat, a, b)


def run_product(slots, virt, pair, aux, *gathered):
    nat = 8 * slots
    return pl.pallas_call(
        functools.partial(product_kernel, slots),
        out_shape=shape(2, 8, packed_rows(slots), 128),
        in_specs=smem(3) + vmem(6),
        out_specs=vmem(1)[0],
        scratch_shapes=[
            pltpu.VMEM((2, TILE, nat), F32),
            pltpu.VMEM((2, TILE, nat), F32),
            pltpu.VMEM((2, 2 * HALF, nat), F32),
            pltpu.VMEM((256, nat), BF16),
            pltpu.VMEM((256, nat), BF16),
            pltpu.SMEM((slots,), I32),
            pltpu.SMEM((8,), I32),
        ],
        compiler_params=pltpu.CompilerParams(vmem_limit_bytes=(20 if slots == SLOTS else 36) * MIB),
    )(virt, pair, aux, *gathered)


def run_scatter(slots, virt, pair, z):
    return pl.pallas_call(
        functools.partial(scatter_kernel, slots),
        out_shape=shape(121, 128),
        in_specs=smem(2) + vmem(1),
        out_specs=vmem(1)[0],
        scratch_shapes=[
            pltpu.VMEM((2, 8, packed_rows(slots), 128), F32),
            pltpu.VMEM((2 * HALF, 128), F32),
            pltpu.VMEM((2 * HALF, 128), F32),
            pltpu.SemaphoreType.DMA((16,)),
            pltpu.SemaphoreType.DMA((16,)),
            pltpu.SemaphoreType.DMA((1,)),
        ],
        compiler_params=pltpu.CompilerParams(
            collective_id=1 if slots == SLOTS else 3, has_side_effects=True, vmem_limit_bytes=16 * MIB
        ),
    )(virt, pair, z)


def packed_path(slots, amplitudes, aux_factor, virt, pair, aux, pat):
    gathered = run_gather(
        slots, virt, pair, aux, pat, amplitudes.reshape(242, 1, 128), aux_factor.reshape(968, 128)
    )
    z = run_product(slots, virt, pair, aux, *gathered)
    return run_scatter(slots, virt, pair, z).reshape(1, 1, 1, TILE * WIDE)


def choose_kernel(virt, out_ref):
    group = iota((8, 1), 0)
    lane = iota((8, 128), 1)
    totals = jnp.zeros((8, 128), I32)
    for b in range(BLOCKS):
        share = cols_before(BLOCK_WIDTH * (b + 1), group) - cols_before(BLOCK_WIDTH * b, group)
        totals = totals + jnp.where(lane == virt[b], share, 0)
    widest = jnp.max(totals)
    out_ref[0] = jnp.where(widest > SLOTS, 1, 0) + jnp.where(widest > 128, 1, 0)


def choose(virt):
    return pl.pallas_call(
        choose_kernel,
        out_shape=jax.ShapeDtypeStruct((1,), I32),
        in_specs=smem(1),
        out_specs=smem(1)[0],
    )(virt)[0]


def block_onehot(indices, block_count):
    return indices[..., None] // BLOCK_WIDTH == jnp.arange(block_count, dtype=jnp.int32)


def label_lookup(hot_table, virt_irrep):
    return jnp.sum(jnp.where(hot_table, virt_irrep, 0), axis=-1)


def gather_along(x, name, axis):
    copies = jnp.broadcast_to(x[None], (lax.axis_size(name), *x.shape))
    parts = jnp.moveaxis(lax.all_to_all(copies, name, 0, 0, tiled=True), 0, axis)
    return parts.reshape(*x.shape[:axis], -1, *x.shape[axis + 1 :])


def sum_scatter(x, name):
    parts = x.reshape(lax.axis_size(name), -1, *x.shape[1:])
    return jnp.sum(lax.all_to_all(parts, name, 0, 0, tiled=True), axis=0)


def dense_path(amplitudes, aux_factor, virt_irrep, pair_irrep, aux_irrep, block_pattern):
    tile_count = lax.axis_size("row")
    col_count = lax.axis_size("col")
    local_rows = VIRTUALS // tile_count
    sub_width = local_rows // col_count
    amplitudes = amplitudes.reshape(amplitudes.shape[0], local_rows, tile_count, sub_width)
    aux_factor = aux_factor.reshape(aux_factor.shape[0], local_rows, tile_count, sub_width)
    block_count = virt_irrep.shape[0]
    row_index = lax.axis_index("row") * local_rows + jnp.arange(local_rows, dtype=jnp.int32)
    col_index = (
        jnp.arange(tile_count, dtype=jnp.int32)[:, None] * local_rows
        + lax.axis_index("col") * sub_width
        + jnp.arange(sub_width, dtype=jnp.int32)[None, :]
    )
    row_hot = block_onehot(row_index, block_count)
    col_hot = block_onehot(col_index, block_count)
    product = jnp.bitwise_xor(
        label_lookup(row_hot, virt_irrep)[:, None, None], label_lookup(col_hot, virt_irrep)[None]
    )
    kept_mask = product[None] == pair_irrep[:, None, None, None]
    masked = jnp.where(kept_mask, amplitudes, 0.0)
    pattern = (block_pattern * block_pattern.T).astype(jnp.float32)
    screen = (
        jnp.einsum(
            "ak,kl,itl->ait", row_hot.astype(jnp.float32), pattern, col_hot.astype(jnp.float32)
        )
        > 0.5
    )
    aux_here = aux_factor.shape[0]
    aux_labels = lax.dynamic_slice_in_dim(aux_irrep, lax.axis_index("occ") * aux_here, aux_here, 0)
    aux_mask = jnp.logical_and(screen[None], product[None] == aux_labels[:, None, None, None])
    factor = jnp.where(aux_mask, aux_factor, 0.0)
    half_pairs = masked.shape[0] // lax.axis_size("occ")
    masked = lax.dynamic_slice_in_dim(masked, lax.axis_index("occ") * half_pairs, half_pairs, 0)
    factor = gather_along(factor, "occ", 0)
    pair_count = masked.shape[0]
    aux_count = factor.shape[0]
    split_view = masked.reshape(pair_count, col_count, sub_width, tile_count, sub_width)
    swapped = lax.all_to_all(
        lax.all_to_all(split_view, "row", split_axis=3, concat_axis=3, tiled=True),
        "col",
        split_axis=1,
        concat_axis=4,
        tiled=True,
    )
    mirrored = swapped.reshape(pair_count, sub_width, tile_count, local_rows).transpose(0, 3, 2, 1)
    antisym = masked - mirrored
    columns = gather_along(factor, "row", 1)
    columns = columns.reshape(aux_count, tile_count, local_rows, tile_count * sub_width)
    rows_panel = gather_along(factor, "col", 3).reshape(
        aux_count, local_rows, tile_count * local_rows
    )
    chosen = columns
    contracted = jnp.einsum(
        "pcik,qikn->qpcn",
        gather_along(antisym, "col", 3),
        chosen,
        precision=lax.Precision.HIGHEST,
    )
    chosen = rows_panel
    partial = jnp.einsum("qca,qpcn->apn", chosen, contracted, precision=lax.Precision.HIGHEST)
    summed = sum_scatter(partial, "row")
    pairs_out = summed.shape[1]
    result = (
        (0.5 * summed).reshape(local_rows, pairs_out, tile_count, sub_width).transpose(1, 0, 2, 3)
    )
    return result.reshape(pairs_out, 1, 1, local_rows * tile_count * sub_width)


def per_device(*args):
    paths = [functools.partial(packed_path, SLOTS), functools.partial(packed_path, 128), dense_path]
    return lax.switch(choose(args[2]), paths, *args)


def solution(mesh):
    placed = (P(None, "row", "col", None), P("occ", "row", "col", None), P(), P(), P(), P())
    return jax.shard_map(
        per_device,
        mesh=mesh,
        in_specs=placed,
        out_specs=P("occ", "row", "col", None),
        check_vma=False,
    )
```

```python
import functools

import jax
import jax.numpy as jnp
from jax import lax
from jax.experimental import pallas as pl
from jax.experimental.pallas import tpu as pltpu
from jax.sharding import PartitionSpec as P

VIRTUALS = 1408
BLOCK_WIDTH = 64
BLOCKS = 22
LABELS = 8
ROWS, COLS = 16, 8
TILE = 88
WIDE = 176
STRIPS = 11
SLOTS = 64
HALF = 48
MESH = pl.DeviceIdType.MESH
MIB = 1 << 20
F32, BF16, I32 = jnp.float32, jnp.bfloat16, jnp.int32


def coords():
    return lax.axis_index("row"), lax.axis_index("col"), lax.axis_index("occ")


def iota(shape, dim):
    return lax.broadcasted_iota(I32, shape, dim)


def div11(v):
    return (v * 5958) >> 16


def split(x):
    hi = x.astype(BF16)
    return hi, (x - hi.astype(F32)).astype(BF16)


def packed_rows(slots):
    return HALF if slots == SLOTS else TILE


def dot_nn(a, b):
    return lax.dot_general(a, b, (((1,), (0,)), ((), ())), preferred_element_type=F32)


def dot_nt(a, b):
    return lax.dot_general(a, b, (((1,), (1,)), ((), ())), preferred_element_type=F32)


def cols_before(n, s):
    return (n // TILE) * STRIPS + jnp.clip(n % TILE - STRIPS * s, 0, STRIPS)


def column_facts(virt, s, shape):
    w = iota(shape, 1)
    d = w + 77 * div11(w) + STRIPS * s
    block = d >> 6
    before = [cols_before(BLOCK_WIDTH * b, s) for b in range(BLOCKS + 1)]
    labels = [virt[b] for b in range(BLOCKS)]
    label = jnp.zeros(shape, I32)
    rank = w
    for b in range(BLOCKS):
        base = -before[b]
        for e in range(b):
            base = base + jnp.where(labels[e] == labels[b], before[e + 1] - before[e], 0)
        here = block == b
        label = jnp.where(here, labels[b], label)
        rank = jnp.where(here, w + base, rank)
    return d, block, label, rank


def row_label(virt, block, first):
    label = virt[first]
    for k in (1, 2):
        label = jnp.where(block == first + k, virt[jnp.minimum(first + k, BLOCKS - 1)], label)
    return label


def pack_tiles(slots, virt, pair, aux, pat, a_ref, b_ref, d_ref, packed, send_a, send_b):
    r, s, o = coords()
    first = (STRIPS * r) >> 3
    d, block, label, rank = column_facts(virt, s, (1, WIDE))
    sel = jnp.where((iota((128, WIDE), 0) & (slots - 1)) == rank, 1.0, 0.0).astype(BF16)
    left = iota((HALF, 128), 1) < SLOTS

    def pack(src, count, keep, base):
        n = count * STRIPS
        if len(src.shape) == 3:
            lines = [src[pl.ds(k, n, stride=STRIPS), 0, :] for k in range(STRIPS)]
        else:
            lines = [src[pl.ds(k, n, stride=STRIPS), :] for k in range(STRIPS)]
        for v in range(8):
            start = WIDE * v
            low, off = start // 128, start % 128
            last = (start + WIDE - 1) // 128
            tile = jnp.concatenate(lines[low : last + 1], axis=1)[:, off : off + WIDE]
            hi, lo = split(jnp.where(keep, tile, 0.0))
            d_ref[pl.ds(v, n, stride=8), :] = dot_nt(hi, sel) + dot_nt(lo, sel)
        d_ref[n * 8 : n * 8 + 8, :] = jnp.zeros((8, 128), F32)
        for k in range(count):
            if slots == SLOTS:
                top = d_ref[pl.ds(TILE * k, HALF), :]
                bottom = d_ref[pl.ds(TILE * k + HALF, HALF), :]
                packed[base + k] = jnp.where(left, top, bottom)
            else:
                packed[base + k] = d_ref[pl.ds(TILE * k, TILE), :]

    row = iota((2 * STRIPS, 1), 0)
    p = jnp.where(row >= STRIPS, 1, 0)
    row_block = (STRIPS * r + row - STRIPS * p) >> 3
    keep = label == (row_label(virt, row_block, first) ^ jnp.where(p == 1, pair[1], pair[0]))
    pack(a_ref, 2, keep, 8)
    send_a()

    screens = []
    for k in range(3):
        x = jnp.minimum(first + k, BLOCKS - 1)
        flag = jnp.zeros((1, WIDE), I32)
        for b in range(BLOCKS):
            flag = jnp.where(block == b, pat[x, b] * pat[b, x], flag)
        screens.append(flag)
    row = iota((TILE, 1), 0)
    q = div11(row)
    row_block = (STRIPS * r + row - STRIPS * q) >> 3
    aux_row = jnp.zeros((TILE, 1), I32)
    for k in range(8):
        aux_row = jnp.where(q == k, aux[8 * o + k], aux_row)
    screen = jnp.where(
        row_block == first, screens[0], jnp.where(row_block == first + 1, screens[1], screens[2])
    )
    target = row_label(virt, row_block, first) ^ aux_row
    pack(b_ref, 8, jnp.logical_and(label == target, screen > 0), 0)
    send_b()


def to_natural(slots, x, target, label, spread, pick):
    hi, lo = split(x)
    both = jnp.concatenate([hi, lo], axis=0)
    target = jnp.concatenate([target, target], axis=0)
    total = jnp.zeros((both.shape[0], 8 * slots), F32)
    for k in range(8):
        j = (slots * k) // 128
        dense = dot_nn(both[:, 128 * j : 128 * j + 128], spread[k])
        dense = jnp.where(label[k : k + 1] == target, dense, 0.0).astype(BF16)
        total = total + dot_nt(dense, pick[k])
    return total[: x.shape[0]] + total[x.shape[0] :]


def my_tiles(r):
    tiles = (r % 8, 8 + r % 8)
    bases = [pl.multiple_of(t * TILE, 8) for t in tiles]
    firsts = [(STRIPS * t) >> 3 for t in tiles]
    row_blocks = [(t * TILE + iota((TILE, 1), 0)) >> 6 for t in tiles]
    return tiles, bases, firsts, row_blocks


def tile_labels(virt, firsts, row_blocks):
    return jnp.concatenate([row_label(virt, b, f) for b, f in zip(row_blocks, firsts)], axis=0)


def gather_kernel(
    slots,
    virt,
    pair,
    aux,
    pat,
    a_ref,
    b_ref,
    a2,
    s2,
    own_natural,
    label_ref,
    spread_ref,
    pick_ref,
    aa_ref,
    sa_ref,
    a_lines,
    d_ref,
    packed,
    send,
    recv,
    near,
):
    r, s, o = coords()
    c, x, y = r % 2, (r // 2) % 4, r // 8

    def at(cc, xx, yy, ss):
        return (yy * 8 + xx * 2 + cc, ss, o)

    zs = {k: at(c, x, y, (s + k) % 8) for k in range(1, 8)}
    planes = {
        (e, k): at(c, (x + k) % 4, (y + e) % 2, s) for e in range(2) for k in range(4) if e + k
    }
    sibling = at(1 - c, x, y, s)
    barrier = pltpu.get_barrier_semaphore()
    for peer in [*zs.values(), *planes.values(), sibling]:
        pl.semaphore_signal(barrier, inc=1, device_id=peer, device_id_type=MESH)

    kinds = {}
    copies = []

    def number(kind):
        return kinds.setdefault(kind, len(kinds))

    def describe(src, dst, peer, kind):
        n = number(kind)
        return pltpu.make_async_remote_copy(
            src_ref=src,
            dst_ref=dst,
            send_sem=send.at[n],
            recv_sem=recv.at[n],
            device_id=peer,
            device_id_type=MESH,
        )

    def put(src, dst, peer, *kind):
        copies.append(describe(src, dst, peer, kind))
        copies[-1].start()

    def arrived(ref, *kind):
        describe(ref, ref, sibling, kind).wait_recv()

    def share(ref, *kind):
        put(ref, ref, sibling, "core", *kind)

    def sign(way, k):
        return k if way else -k

    def a_block(k, ch, cc=c):
        return aa_ref.at[cc, 2 * ch : 2 * ch + 2, :, (s + k + 8) % 8]

    def s_block(k, e, cc=c):
        return sa_ref.at[cc, (x + k + 4) % 4, (y + e) % 2]

    def send_a():
        pl.semaphore_wait(barrier, 15)
        for (e, k), peer in planes.items():
            put(packed.at[8 + (y + e) % 2], aa_ref.at[c, x, y, s], peer, "ax", e, k)
        own = pltpu.make_async_copy(packed.at[8 + y], aa_ref.at[c, x, y, s], near.at[0])
        own.start()
        own.wait()

    def send_b():
        for k in (4, 3, 5, 2, 6, 1, 7):
            put(packed.at[(s + k) % 8], sa_ref.at[c, x, y, s], zs[k], "sz", k)
        own = pltpu.make_async_copy(packed.at[s], sa_ref.at[c, x, y, s], near.at[1])
        own.start()
        own.wait()

    amplitudes = pltpu.make_async_copy(a_ref, a_lines, near.at[2])
    amplitudes.start()
    amplitudes.wait()
    pack_tiles(slots, virt, pair, aux, pat, a_lines, b_ref, d_ref, packed, send_a, send_b)

    def tile_base(xx, yy, cc):
        return pl.multiple_of((yy * 8 + xx * 2 + cc) * TILE, 8)

    half_lanes = iota((HALF, 128), 1) < SLOTS

    def take_a(k, ch, cc=c):
        ss = (s + k + 8) % 8
        lane = pl.multiple_of(128 * (ss // (128 // slots)), 128)

        def take(n, _):
            xx, yy = 2 * ch + n // 2, n % 2
            base = tile_base(xx, yy, cc)
            piece = aa_ref[cc, xx, yy, ss]
            if slots != SLOTS:
                a2[pl.ds(base, TILE), pl.ds(lane, 128)] = piece
                return 0
            low = pl.ds(base, HALF)
            high = pl.ds(pl.multiple_of(base + HALF, 8), TILE - HALF)
            rest = half_lanes[: TILE - HALF]
            lanes = pl.ds(lane, 128)

            @pl.when(ss % 2 == 0)
            def _():
                turned = pltpu.roll(piece[: TILE - HALF], SLOTS, 1)
                a2[low, lanes] = jnp.where(half_lanes, piece, a2[low, lanes])
                a2[high, lanes] = jnp.where(rest, turned, a2[high, lanes])

            @pl.when(ss % 2 == 1)
            def _():
                turned = pltpu.roll(piece, SLOTS, 1)
                a2[low, lanes] = jnp.where(half_lanes, a2[low, lanes], turned)
                a2[high, lanes] = jnp.where(rest, a2[high, lanes], piece[: TILE - HALF])

            return 0

        lax.fori_loop(0, 4, take, 0)

    def take_s(k, e, cc=c):
        xx, yy = (x + k + 4) % 4, (y + e) % 2
        base = tile_base(xx, yy, cc)
        if slots != SLOTS:
            for j in range(8):
                s2[pl.ds(base, TILE), pl.ds(128 * j, 128)] = sa_ref[cc, xx, yy, j]
            return
        for j in range(4):
            even, odd = sa_ref[cc, xx, yy, 2 * j], sa_ref[cc, xx, yy, 2 * j + 1]
            top = jnp.where(half_lanes, even, pltpu.roll(odd, SLOTS, 1))
            bottom = jnp.where(half_lanes, pltpu.roll(even, SLOTS, 1), odd)
            s2[pl.ds(base, HALF), pl.ds(128 * j, 128)] = top
            s2[pl.ds(base + HALF, TILE - HALF), pl.ds(128 * j, 128)] = bottom[: TILE - HALF]

    def a_ring(h, chs=(0, 1)):
        for ch in chs:
            for way in range(2):
                block = a_block(sign(1 - way, h), ch)
                if h and (h < 4 or ch != way):
                    arrived(block, "az", way, h - 1, ch)
                if h < 3 or (h == 3 and ch != way):
                    put(block, block, zs[1 if way else 7], "az", way, h, ch)
                if h and (h < 4 or ch != way):
                    share(block, "az", way, h - 1, ch)
                if h == 0 and way == 0:
                    share(block, "own", ch)

    def a_take(h):
        for ch in range(2):
            for way in range(2):
                if (h and (h < 4 or ch != way)) or (h == 0 and way == 0):
                    take_a(sign(1 - way, h), ch)

    def a_sibling(h):
        for ch in range(2):
            if h == 0:
                arrived(a_block(0, ch, 1 - c), "core", "own", ch)
                take_a(0, ch, 1 - c)
                continue
            for way in range(2):
                if h < 4 or ch != way:
                    k = sign(1 - way, h)
                    arrived(a_block(k, ch, 1 - c), "core", "az", way, h - 1, ch)
                    take_a(k, ch, 1 - c)

    def s_arrival(e):
        for way in range(2):
            block = s_block(sign(1 - way, 1), e)
            arrived(block, "sx", way, e)
            if e != way:
                put(block, block, planes[0, 1 if way else 3], "sxx", way)
            share(block, "sx", way, e)

    def s_take(e):
        for way in range(2):
            take_s(sign(1 - way, 1), e)

    def s_sibling(e):
        for way in range(2):
            k = sign(1 - way, 1)
            arrived(s_block(k, e, 1 - c), "core", "sx", way, e)
            take_s(k, e, 1 - c)

    def s_start(e):
        block = s_block(0, e)
        for way in range(2):
            put(block, block, planes[0, 1 if way else 3], "sx", way, e)
        share(block, "sy", e)

    def s_start_sibling(e):
        arrived(s_block(0, e, 1 - c), "core", "sy", e)
        take_s(0, e, 1 - c)

    for e, k in planes:
        arrived(aa_ref.at[c, (x - k + 4) % 4, (y + e) % 2, s], "ax", e, k)
    a_ring(0, (0,))

    group = iota((8, 1), 0)
    d, block, label, rank = column_facts(virt, group, (8, WIDE))
    place = jnp.zeros((8, WIDE), I32)
    for b in range(BLOCKS):
        seen = 0
        for e in range(b):
            seen = seen + jnp.where(virt[e] == virt[b], 1, 0)
        place = jnp.where(block == b, seen, place)
    natural = place * BLOCK_WIDTH + (d & (BLOCK_WIDTH - 1))
    label_ref[...] = label
    for k in range(8):
        shift = (slots * k) % 128
        spread = jnp.where(iota((128, WIDE), 0) == rank[k : k + 1] + shift, 1.0, 0.0)
        spread_ref[k] = spread.astype(BF16)
    a2[...] = jnp.zeros_like(a2)
    s2[VIRTUALS:, :] = jnp.zeros((BLOCK_WIDTH, 8 * slots), F32)

    def build_picks(ks):
        for k in ks:
            pick = jnp.where(iota((8 * slots, WIDE), 0) == natural[k : k + 1], 1.0, 0.0)
            pick_ref[k] = pick.astype(BF16)

    a_ring(0, (1,))
    build_picks(range(4))
    for k in (1, 7, 2, 6, 3, 5, 4):
        arrived(sa_ref.at[c, x, y, (s - k + 8) % 8], "sz", k)
    put(s_block(0, 0), s_block(0, 0), planes[1, 0], "sy")
    s_start(0)
    a_take(0)
    take_s(0, 0)
    build_picks(range(4, 8))
    a_ring(1, (0,))
    arrived(s_block(0, 1), "sy")
    s_start(1)
    a_ring(1, (1,))
    take_s(0, 1)
    tiles, bases, firsts, row_blocks = my_tiles(r)
    target = tile_labels(virt, firsts, row_blocks) ^ aux[8 * o + s]
    own = jnp.concatenate([s2[pl.ds(b, TILE), :] for b in bases], axis=0)
    own_natural[...] = to_natural(slots, own, target, label, spread_ref, pick_ref)
    s_arrival(0)
    a_ring(2, (0,))
    a_take(1)
    s_start_sibling(0)
    s_start_sibling(1)
    a_ring(2, (1,))
    s_take(0)
    a_sibling(0)
    a_sibling(1)
    s_arrival(1)
    a_ring(3, (0,))
    a_take(2)
    s_take(1)
    a_ring(3, (1,))
    a_take(3)
    s_sibling(0)
    a_sibling(2)
    for way in range(2):
        block = s_block(2, 1 - way)
        arrived(block, "sxx", way)
        share(block, "sxx", way)
    a_ring(4)
    s_sibling(1)
    a_sibling(3)
    for way in range(2):
        take_s(2, 1 - way)
    a_take(4)
    for way in range(2):
        arrived(s_block(2, 1 - way, 1 - c), "core", "sxx", way)
        take_s(2, 1 - way, 1 - c)
    a_sibling(4)
    for copy in copies:
        copy.wait_send()


def product_kernel(
    slots,
    virt,
    pair,
    aux,
    a2,
    s2,
    own_natural,
    label_ref,
    spread_ref,
    pick_ref,
    z_ref,
    v1,
    v2,
    zs,
    whi,
    wlo,
    lists,
    counts,
):
    r, s, o = coords()
    nat, per_label = 8 * slots, slots // 8
    h = aux[8 * o + s]
    hp = h ^ pair[r // 8]
    left = iota((HALF, 128), 1) < SLOTS
    for g in range(LABELS):
        counts[g] = 0
        for j in range(per_label):
            lists[per_label * g + j] = BLOCKS
    for b in range(BLOCKS):
        g = virt[b]
        n = counts[g]
        lists[per_label * g + jnp.minimum(n, per_label - 1)] = b
        counts[g] = n + 1
    tiles, bases, firsts, row_blocks = my_tiles(r)
    labels = tile_labels(virt, firsts, row_blocks)

    def load_rows(src, g, half):
        for j in range(4):
            b = lists[per_label * g + 4 * half + j]
            hi, lo = split(src[pl.ds(pl.multiple_of(b * BLOCK_WIDTH, BLOCK_WIDTH), BLOCK_WIDTH), :])
            whi[pl.ds(BLOCK_WIDTH * j, BLOCK_WIDTH), :] = hi
            wlo[pl.ds(BLOCK_WIDTH * j, BLOCK_WIDTH), :] = lo

    def dot3(dot, a):
        tall = 2 * HALF
        hi, lo = split(jnp.concatenate([a, jnp.zeros((tall - TILE, a.shape[1]), F32)], axis=0))
        both = dot(jnp.concatenate([hi, lo], axis=0), whi[...])
        return (both[:tall] + both[tall:] + dot(hi, wlo[...]))[:TILE]

    v1[...] = jnp.zeros_like(v1)
    v2[...] = jnp.zeros_like(v2)
    zs[...] = jnp.zeros_like(zs)
    for t in range(2):
        last = (STRIPS * tiles[t] + STRIPS - 1) >> 3

        def first_product(x, _, t=t):
            g1 = virt[x] ^ h
            g2 = virt[x] ^ hp
            here = row_blocks[t] == x
            mine = jnp.where(here, s2[pl.ds(bases[t], TILE), :], 0.0)
            mine_natural = jnp.where(here, own_natural[TILE * t : TILE * t + TILE, :], 0.0)
            for half in range(nat // 256):
                part = slice(256 * half, 256 * half + 256)

                @pl.when(counts[g1] > 4 * half)
                def _():
                    load_rows(a2, g1, half)
                    v2[t] += dot3(dot_nn, mine_natural[:, part])

                @pl.when(counts[g2] > 4 * half)
                def _():
                    load_rows(a2, g2, half)
                    v1[t, :, part] += dot3(dot_nt, mine)

            return 0

        lax.fori_loop(firsts[t], last + 1, first_product, 0)

    v2_rows = jnp.concatenate([v2[0], v2[1]], axis=0)
    turned = to_natural(slots, v2_rows, labels ^ hp, label_ref[...], spread_ref, pick_ref)
    for t in range(2):
        last = (STRIPS * tiles[t] + STRIPS - 1) >> 3
        y = turned[TILE * t : TILE * t + TILE] - v1[t]

        def second_product(x, _, t=t, y=y):
            g2 = virt[x] ^ hp
            mine = jnp.where(row_blocks[t] == x, y, 0.0)
            for half in range(nat // 256):

                @pl.when(counts[g2] > 4 * half)
                def _():
                    load_rows(s2, g2, half)
                    zs[t, :TILE] += dot3(dot_nn, mine[:, 256 * half : 256 * half + 256])

            return 0

        lax.fori_loop(firsts[t], last + 1, second_product, 0)

    for t in range(2):
        for k in range(8):
            if slots != SLOTS:
                z_ref[t, k] = zs[t, :TILE, pl.ds(128 * k, 128)]
                continue
            j = k // 2
            top = zs[t, 0:HALF, pl.ds(128 * j, 128)]
            bottom = zs[t, HALF : 2 * HALF, pl.ds(128 * j, 128)]
            if k % 2 == 0:
                z_ref[t, k] = jnp.where(left, top, pltpu.roll(bottom, SLOTS, 1))
            else:
                z_ref[t, k] = jnp.where(left, pltpu.roll(top, SLOTS, 1), bottom)


def scatter_kernel(slots, virt, pair, z_ref, out_ref, parts, low_ref, high_ref, send, recv, near):
    r, s, o = coords()
    y, rest = r // 8, r % 8
    alone = jnp.where(y == o, 1, 0)
    barrier = pltpu.get_barrier_semaphore()

    def greet(e, k):
        pl.semaphore_signal(
            barrier, inc=1, device_id=(o * 8 + rest, (s + k) % 8, e), device_id_type=MESH
        )

    def describe(e, k):
        return pltpu.make_async_remote_copy(
            src_ref=z_ref.at[e, (s + k) % 8],
            dst_ref=parts.at[o, s],
            send_sem=send.at[8 * e + k],
            recv_sem=recv.at[8 * o + k],
            device_id=(e * 8 + rest, (s + k) % 8, y),
            device_id_type=MESH,
        )

    def sender(e, k):
        describe(e, k).start()

    def receive(e, k):
        spot = parts.at[e, (s - k + 8) % 8]
        pltpu.make_async_remote_copy(
            src_ref=spot,
            dst_ref=spot,
            send_sem=send.at[0],
            recv_sem=recv.at[8 * e + k],
            device_id=(o * 8 + rest, (s + 1) % 8, e),
            device_id_type=MESH,
        ).wait_recv()

    def finish(e, k):
        describe(e, k).wait_send()

    def each(fn, mine):
        for k in (4, 3, 5, 2, 6, 1, 7, 0):
            for e in range(2):
                if k:
                    fn(e, k)
                else:
                    pl.when(jnp.logical_or(y != o, mine != e))(functools.partial(fn, e, k))

    each(greet, o)
    pl.semaphore_wait(barrier, 16 - alone)
    each(sender, y)

    @pl.when(y == o)
    def _():
        copy = pltpu.make_async_copy(z_ref.at[y, s], parts.at[o, s], near.at[0])
        copy.start()
        copy.wait()

    first = (STRIPS * r) >> 3
    d, block, label, rank = column_facts(virt, s, (1, WIDE))
    each(receive, o)
    total = parts[0, 0]
    for k in range(1, 16):
        total = total + parts[k // 8, k % 8]
    hi, lo = split(0.5 * total)
    rows = packed_rows(slots)
    row = iota((rows, 1), 0)
    for half in range(128 // slots):
        spread = jnp.where(iota((128, WIDE), 0) == rank + slots * half, 1.0, 0.0).astype(BF16)
        dense = dot_nn(hi, spread) + dot_nn(lo, spread)
        row_block = (TILE * r + rows * half + row) >> 6
        keep = label == (row_label(virt, row_block, first) ^ pair[o])
        dense = jnp.where(keep, dense, 0.0)
        low_ref[rows * half : rows * half + rows, :] = dense[:, :128]
        high_ref[rows * half : rows * half + rows, :] = jnp.concatenate(
            [dense[:, 128:], jnp.zeros((rows, 256 - WIDE), F32)], axis=1
        )
    lines = []
    for v in range(8):
        low, high = low_ref[pl.ds(v, STRIPS, stride=8), :], high_ref[pl.ds(v, STRIPS, stride=8), :]
        lines.append(jnp.concatenate([low, high[:, : WIDE - 128]], axis=1))
    for k in range(STRIPS):
        v, w = (128 * k) // WIDE, (128 * k) % WIDE
        piece = lines[v][:, w : min(WIDE, w + 128)]
        if w + 128 > WIDE:
            piece = jnp.concatenate([piece, lines[v + 1][:, : w + 128 - WIDE]], axis=1)
        out_ref[pl.ds(k, STRIPS, stride=STRIPS), :] = piece
    each(finish, y)


def smem(n):
    return [pl.BlockSpec(memory_space=pltpu.SMEM)] * n


def vmem(n):
    return [pl.BlockSpec(memory_space=pltpu.VMEM)] * n


def shape(*dims):
    return jax.ShapeDtypeStruct(dims, F32)


def run_gather(slots, virt, pair, aux, pat, a, b):
    rows, nat = packed_rows(slots), 8 * slots
    full = pltpu.VMEM((2, 4, 2, 8, rows, 128), F32)
    return pl.pallas_call(
        functools.partial(gather_kernel, slots),
        out_shape=(
            shape(VIRTUALS + BLOCK_WIDTH, nat),
            shape(VIRTUALS + BLOCK_WIDTH, nat),
            shape(WIDE, nat),
            jax.ShapeDtypeStruct((8, WIDE), I32),
            jax.ShapeDtypeStruct((8, 128, WIDE), BF16),
            jax.ShapeDtypeStruct((8, nat, WIDE), BF16),
        ),
        in_specs=smem(4) + [pl.BlockSpec(memory_space=pl.ANY)] + vmem(1),
        out_specs=tuple(vmem(6)),
        scratch_shapes=[
            full,
            full,
            pltpu.VMEM((2 * 121, 1, 128), F32),
            pltpu.VMEM((8 * TILE + 8, 128), F32),
            pltpu.VMEM((10, rows, 128), F32),
            pltpu.SemaphoreType.DMA((64,)),
            pltpu.SemaphoreType.DMA((64,)),
            pltpu.SemaphoreType.DMA((3,)),
        ],
        compiler_params=pltpu.CompilerParams(
            collective_id=0 if slots == SLOTS else 2,
            has_side_effects=True,
            vmem_limit_bytes=(20 if slots == SLOTS else 36) * MIB,
        ),
    )(virt, pair, aux, pat, a, b)


def run_product(slots, virt, pair, aux, *gathered):
    nat = 8 * slots
    return pl.pallas_call(
        functools.partial(product_kernel, slots),
        out_shape=shape(2, 8, packed_rows(slots), 128),
        in_specs=smem(3) + vmem(6),
        out_specs=vmem(1)[0],
        scratch_shapes=[
            pltpu.VMEM((2, TILE, nat), F32),
            pltpu.VMEM((2, TILE, nat), F32),
            pltpu.VMEM((2, 2 * HALF, nat), F32),
            pltpu.VMEM((256, nat), BF16),
            pltpu.VMEM((256, nat), BF16),
            pltpu.SMEM((slots,), I32),
            pltpu.SMEM((8,), I32),
        ],
        compiler_params=pltpu.CompilerParams(vmem_limit_bytes=(20 if slots == SLOTS else 36) * MIB),
    )(virt, pair, aux, *gathered)


def run_scatter(slots, virt, pair, z):
    return pl.pallas_call(
        functools.partial(scatter_kernel, slots),
        out_shape=shape(121, 128),
        in_specs=smem(2) + vmem(1),
        out_specs=vmem(1)[0],
        scratch_shapes=[
            pltpu.VMEM((2, 8, packed_rows(slots), 128), F32),
            pltpu.VMEM((2 * HALF, 128), F32),
            pltpu.VMEM((2 * HALF, 128), F32),
            pltpu.SemaphoreType.DMA((16,)),
            pltpu.SemaphoreType.DMA((16,)),
            pltpu.SemaphoreType.DMA((1,)),
        ],
        compiler_params=pltpu.CompilerParams(
            collective_id=1 if slots == SLOTS else 3, has_side_effects=True, vmem_limit_bytes=16 * MIB
        ),
    )(virt, pair, z)


def packed_path(slots, amplitudes, aux_factor, virt, pair, aux, pat):
    gathered = run_gather(
        slots, virt, pair, aux, pat, amplitudes.reshape(242, 1, 128), aux_factor.reshape(968, 128)
    )
    z = run_product(slots, virt, pair, aux, *gathered)
    return run_scatter(slots, virt, pair, z).reshape(1, 1, 1, TILE * WIDE)


def choose_kernel(virt, out_ref):
    group = iota((8, 1), 0)
    lane = iota((8, 128), 1)
    totals = jnp.zeros((8, 128), I32)
    for b in range(BLOCKS):
        share = cols_before(BLOCK_WIDTH * (b + 1), group) - cols_before(BLOCK_WIDTH * b, group)
        totals = totals + jnp.where(lane == virt[b], share, 0)
    widest = jnp.max(totals)
    out_ref[0] = jnp.where(widest > SLOTS, 1, 0) + jnp.where(widest > 128, 1, 0)


def choose(virt):
    return pl.pallas_call(
        choose_kernel,
        out_shape=jax.ShapeDtypeStruct((1,), I32),
        in_specs=smem(1),
        out_specs=smem(1)[0],
    )(virt)[0]


def block_onehot(indices, block_count):
    return indices[..., None] // BLOCK_WIDTH == jnp.arange(block_count, dtype=jnp.int32)


def label_lookup(hot_table, virt_irrep):
    return jnp.sum(jnp.where(hot_table, virt_irrep, 0), axis=-1)


def gather_along(x, name, axis):
    copies = jnp.broadcast_to(x[None], (lax.axis_size(name), *x.shape))
    parts = jnp.moveaxis(lax.all_to_all(copies, name, 0, 0, tiled=True), 0, axis)
    return parts.reshape(*x.shape[:axis], -1, *x.shape[axis + 1 :])


def sum_scatter(x, name):
    parts = x.reshape(lax.axis_size(name), -1, *x.shape[1:])
    return jnp.sum(lax.all_to_all(parts, name, 0, 0, tiled=True), axis=0)


def dense_path(amplitudes, aux_factor, virt_irrep, pair_irrep, aux_irrep, block_pattern):
    tile_count = lax.axis_size("row")
    col_count = lax.axis_size("col")
    local_rows = VIRTUALS // tile_count
    sub_width = local_rows // col_count
    amplitudes = amplitudes.reshape(amplitudes.shape[0], local_rows, tile_count, sub_width)
    aux_factor = aux_factor.reshape(aux_factor.shape[0], local_rows, tile_count, sub_width)
    block_count = virt_irrep.shape[0]
    row_index = lax.axis_index("row") * local_rows + jnp.arange(local_rows, dtype=jnp.int32)
    col_index = (
        jnp.arange(tile_count, dtype=jnp.int32)[:, None] * local_rows
        + lax.axis_index("col") * sub_width
        + jnp.arange(sub_width, dtype=jnp.int32)[None, :]
    )
    row_hot = block_onehot(row_index, block_count)
    col_hot = block_onehot(col_index, block_count)
    product = jnp.bitwise_xor(
        label_lookup(row_hot, virt_irrep)[:, None, None], label_lookup(col_hot, virt_irrep)[None]
    )
    kept_mask = product[None] == pair_irrep[:, None, None, None]
    masked = jnp.where(kept_mask, amplitudes, 0.0)
    pattern = (block_pattern * block_pattern.T).astype(jnp.float32)
    screen = (
        jnp.einsum(
            "ak,kl,itl->ait", row_hot.astype(jnp.float32), pattern, col_hot.astype(jnp.float32)
        )
        > 0.5
    )
    aux_here = aux_factor.shape[0]
    aux_labels = lax.dynamic_slice_in_dim(aux_irrep, lax.axis_index("occ") * aux_here, aux_here, 0)
    aux_mask = jnp.logical_and(screen[None], product[None] == aux_labels[:, None, None, None])
    factor = jnp.where(aux_mask, aux_factor, 0.0)
    half_pairs = masked.shape[0] // lax.axis_size("occ")
    masked = lax.dynamic_slice_in_dim(masked, lax.axis_index("occ") * half_pairs, half_pairs, 0)
    factor = gather_along(factor, "occ", 0)
    pair_count = masked.shape[0]
    aux_count = factor.shape[0]
    split_view = masked.reshape(pair_count, col_count, sub_width, tile_count, sub_width)
    swapped = lax.all_to_all(
        lax.all_to_all(split_view, "row", split_axis=3, concat_axis=3, tiled=True),
        "col",
        split_axis=1,
        concat_axis=4,
        tiled=True,
    )
    mirrored = swapped.reshape(pair_count, sub_width, tile_count, local_rows).transpose(0, 3, 2, 1)
    antisym = masked - mirrored
    columns = gather_along(factor, "row", 1)
    columns = columns.reshape(aux_count, tile_count, local_rows, tile_count * sub_width)
    rows_panel = gather_along(factor, "col", 3).reshape(
        aux_count, local_rows, tile_count * local_rows
    )
    chosen = columns
    contracted = jnp.einsum(
        "pcik,qikn->qpcn",
        gather_along(antisym, "col", 3),
        chosen,
        precision=lax.Precision.HIGHEST,
    )
    chosen = rows_panel
    partial = jnp.einsum("qca,qpcn->apn", chosen, contracted, precision=lax.Precision.HIGHEST)
    summed = sum_scatter(partial, "row")
    pairs_out = summed.shape[1]
    result = (
        (0.5 * summed).reshape(local_rows, pairs_out, tile_count, sub_width).transpose(1, 0, 2, 3)
    )
    return result.reshape(pairs_out, 1, 1, local_rows * tile_count * sub_width)


def per_device(*args):
    paths = [functools.partial(packed_path, SLOTS), functools.partial(packed_path, 128), dense_path]
    return lax.switch(choose(args[2]), paths, *args)


def solution(mesh):
    placed = (P(None, "row", "col", None), P("occ", "row", "col", None), P(), P(), P(), P())
    return jax.shard_map(
        per_device,
        mesh=mesh,
        in_specs=placed,
        out_specs=P("occ", "row", "col", None),
        check_vma=False,
    )
```
